128 devices in a mesh: row: 16 (over y, z_lo, core), col: 8 (over x, z_hi).
Axes of the slice: x: 4, y: 4, z: 4 (z_hi: 2, z_lo: 2; z = z_hi * 2 + z_lo), core: 2. Of those that a mesh axis runs over, the one named last changes fastest.
Arguments:
- pair: bfloat16 [768, 768, 128], P('row', 'col'), may hold values from -6 to 6
- bins: int32 [768, 768], P('row', 'col'), may hold values from 0 to 14
- mask: int32 [768], replicated, may hold values 0 or 1
- emb_table: bfloat16 [15, 128], replicated, may hold values from -6 to 6
- ln_gain: float32 [128], replicated, may hold values from 0.1 to 1.9
- ln_bias: float32 [128], replicated, may hold values from -3 to 3
- proj_weight: bfloat16 [128, 512], replicated, may hold values from -0.5 to 0.5
- gate_weight: bfloat16 [128, 128], replicated, may hold values from -0.5 to 0.5
- norm_gain: float32 [128], replicated, may hold values from 0.1 to 1.9
- norm_bias: float32 [128], replicated, may hold values from -3 to 3
- out_weight: bfloat16 [128, 128], replicated, may hold values from -0.5 to 0.5
Outputs:
- pair_out: bfloat16 [768, 768, 128], P('row', 'col')
The draws below stay inside these ranges and needn't reach their ends.
All inputs are finite; a program needn't handle non-finite values.
Results may differ from the reference program's by a relative error of at most 0.0085.
Values may be sent and summed in bfloat16 or wider, within the bound.
No kernel may reach another device: no remote copies, remote signals or barrier semaphores. Data moves between devices by JAX's collectives and lax.ppermute only.
A program may use at most 128 MiB of HBM per device.

```python
import jax
import jax.numpy as jnp
from jax import lax

C_Z = 128
HID = 128
BINS = 15
RES = 768


def with_ends(array, own_key, smallest, largest):
    extent = array.shape
    place = [jax.random.randint(jax.random.fold_in(own_key, axis), (), 0, extent[axis]) for axis in range(len(extent))]
    array = array.at[tuple(place)].set(smallest)
    longest = extent.index(max(extent))
    place[longest] = (place[longest] + 1) % extent[longest]
    return array.at[tuple(place)].set(largest)


def shard_levels(key, extent, pieces, low, high):
    def one(dim, shards_of):
        heights = jax.random.uniform(jax.random.fold_in(jax.random.fold_in(key, 6), dim), (shards_of,), jnp.float32, low / len(pieces), high / len(pieces))
        return jnp.repeat(jnp.exp(heights), extent[dim] // shards_of).reshape((-1,) + (1,) * (len(extent) - dim - 1))

    level = one(*pieces[0])
    for cut in pieces[1:]:
        level = level * one(*cut)
    return level


def bell_draw(stream_key, extent, spread, limit, shards=(), held_as=jnp.bfloat16):
    values = spread * jax.random.normal(stream_key, extent, jnp.float32)
    if shards:
        values = values * shard_levels(stream_key, extent, shards, -0.22, 0.18)
    return jnp.clip(values, -limit, limit).astype(held_as)


def setup_inputs(seed: int = 0) -> dict:
    arg_keys = jax.random.split(jax.random.key(seed), 12)
    return {
        "pair": bell_draw(arg_keys[0], (RES, RES, C_Z), 1.0, 6.0, ((0, 16), (1, 8))),
        "bins": with_ends(jax.random.randint(arg_keys[1], (RES, RES), 0, BINS), jax.random.fold_in(arg_keys[1], 1), 0, BINS - 1).astype(jnp.int32),
        "mask": with_ends((jax.random.randint(arg_keys[2], (RES,), 0, 10) < 9).astype(jnp.int32), jax.random.fold_in(arg_keys[2], 1), 0, 1),
        "emb_table": bell_draw(arg_keys[3], (BINS, C_Z), 1.0, 6.0),
        "ln_gain": jnp.clip(1.0 + 0.18 * jax.random.normal(arg_keys[4], (C_Z,), jnp.float32), 0.1, 1.9),
        "ln_bias": bell_draw(arg_keys[5], (C_Z,), 0.5, 3.0, (), jnp.float32),
        "proj_weight": bell_draw(arg_keys[6], (C_Z, 4 * HID), C_Z ** -0.5, 0.5),
        "gate_weight": bell_draw(arg_keys[7], (C_Z, C_Z), C_Z ** -0.5, 0.5),
        "norm_gain": jnp.clip(1.0 + 0.18 * jax.random.normal(arg_keys[8], (HID,), jnp.float32), 0.1, 1.9),
        "norm_bias": bell_draw(arg_keys[9], (HID,), 0.5, 3.0, (), jnp.float32),
        "out_weight": bell_draw(arg_keys[10], (HID, C_Z), HID ** -0.5, 0.5),
    }


def layer_norm(values, gain, bias):
    mean = lax.optimization_barrier(jnp.mean(values, axis=-1, keepdims=True))
    centred = values - mean
    var = lax.optimization_barrier(jnp.mean(centred * centred, axis=-1, keepdims=True))
    return centred / jnp.sqrt(var + 1e-05) * gain + bias

def reference(pair, bins, mask, emb_table, ln_gain, ln_bias, proj_weight, gate_weight, norm_gain, norm_bias, out_weight):
    summed = pair.astype(jnp.float32) + emb_table[bins].astype(jnp.float32)
    normed = layer_norm(summed, ln_gain, ln_bias).astype(jnp.bfloat16)
    proj = jnp.dot(normed, proj_weight, preferred_element_type=jnp.float32)
    mask_f = mask.astype(jnp.float32)
    pair_mask = mask_f[:, None, None] * mask_f[None, :, None]
    left = (pair_mask * jax.nn.sigmoid(proj[..., HID:2 * HID]) * proj[..., 0:HID]).astype(jnp.bfloat16)
    right = (pair_mask * jax.nn.sigmoid(proj[..., 3 * HID:4 * HID]) * proj[..., 2 * HID:3 * HID]).astype(jnp.bfloat16)
    gate = jax.nn.sigmoid(jnp.dot(normed, gate_weight, preferred_element_type=jnp.float32))
    tri = jnp.einsum('ikc,jkc->ijc', left.astype(jnp.float32), right.astype(jnp.float32), precision=lax.Precision.HIGHEST)
    tri_normed = layer_norm(tri, norm_gain, norm_bias).astype(jnp.bfloat16)
    update = gate * jnp.dot(tri_normed, out_weight, preferred_element_type=jnp.float32)
    return (summed + update).astype(jnp.bfloat16)
```

```python
import jax
import jax.numpy as jnp
from jax import lax
from jax.experimental import pallas as pl
from jax.experimental.pallas import tpu as pltpu
from jax.sharding import PartitionSpec as P

EPS = 1e-5
F32 = jnp.float32
BF16 = jnp.bfloat16
NT = (((1,), (1,)), ((), ()))
NN = (((1,), (0,)), ((), ()))
VMEM = 48 * 1024 * 1024


def column_rows(col):
    if col < 8:
        return [8 * b + col for b in range(4)]
    p = col - 8
    return [32 + p, 40 + p, 36 + p, 44 + p]


def sigmoid(x):
    return 0.5 * jnp.tanh(0.5 * x) + 0.5


def norm_sublanes(x, gain, bias):
    mean = jnp.mean(x, axis=0, keepdims=True)
    centred = x - mean
    var = jnp.mean(centred * centred, axis=0, keepdims=True)
    return (centred * lax.rsqrt(var + EPS) * gain + bias).astype(BF16)


def dot(a, b, dims=NN):
    return lax.dot_general(a, b, dims, preferred_element_type=F32)


def one_hot_rows(code):
    level = lax.broadcasted_iota(jnp.int32, (16, code.shape[1]), 0)
    return jnp.where((code & 15) == level, 1.0, 0.0).astype(BF16)


def project_kernel(pair, code, eye, emb_t, gain, bias, weight_t, out, normed_out):
    low = lax.broadcasted_iota(jnp.int32, (128, 128), 1) < 64
    for half in range(2):
        gs = [2 * half, 2 * half + 1, 2 * half + 4, 2 * half + 5]
        ps = [2 * half, 2 * half + 1]
        cols = gs + [8 + p for p in ps]
        rows = [pair[i] for c in cols for i in column_rows(c)]
        x = jnp.concatenate(rows, axis=0)
        codes = jnp.concatenate([code[0, c : c + 1, :] for c in cols], axis=1)
        summed = dot(eye[...], x, NT) + dot(emb_t[...], one_hot_rows(codes))
        normed = norm_sublanes(summed, gain[...], bias[...])
        for n, c in enumerate(cols):
            normed_out[0, c] = normed[:, 128 * n : 128 * (n + 1)]
        proj = dot(weight_t[...], normed)
        keep = jnp.where(codes >= 16, 1.0, 0.0)
        left = keep * sigmoid(proj[128:256]) * proj[0:128]
        right = keep * sigmoid(proj[384:512]) * proj[256:384]
        for n, g in enumerate(gs):
            p = 4 + n % 2
            lane = slice(128 * n, 128 * (n + 1))
            tail = slice(128 * p, 128 * (p + 1))
            left_tail, right_tail = left[:, tail], right[:, tail]
            if g < 4:
                left_tail = pltpu.roll(left_tail, 64, 1)
            else:
                right_tail = pltpu.roll(right_tail, 64, 1)
            out[g] = left[:, lane].astype(BF16)
            out[8 + g] = jnp.where(low, right[:, lane], left_tail).astype(BF16)
            out[16 + g] = jnp.where(low, right_tail, right[:, lane]).astype(BF16)


def project(pair, code, eye, emb_t, gain, bias, weight_t):
    whole = lambda a: pl.BlockSpec(a.shape, lambda m: (0,) * a.ndim)
    return pl.pallas_call(
        project_kernel,
        grid=(3,),
        in_specs=[
            pl.BlockSpec((48, 32, 128), lambda m: (0, m, 0)),
            pl.BlockSpec((1, 12, 128), lambda m: (m, 0, 0)),
            whole(eye),
            whole(emb_t),
            whole(gain),
            whole(bias),
            whole(weight_t),
        ],
        out_specs=[
            pl.BlockSpec((24, 128, 128), lambda m: (m, 0, 0)),
            pl.BlockSpec((1, 12, 128, 128), lambda m: (m, 0, 0, 0)),
        ],
        out_shape=[
            jax.ShapeDtypeStruct((72, 128, 128), BF16),
            jax.ShapeDtypeStruct((3, 12, 128, 128), BF16),
        ],
        compiler_params=pltpu.CompilerParams(vmem_limit_bytes=VMEM),
    )(pair, code, eye, emb_t, gain, bias, weight_t)


LEFT_AT = [(0, 0), (0, 1), (0, 2), (0, 3), (1, 2), (1, 3)]
RIGHT_AT = [(1, 0), (1, 1), (2, 2), (2, 3), (2, 0), (2, 1)]


def roll_slots(x, by):
    by %= 4
    return x if by == 0 else pltpu.roll(x, 32 * by, 1)


def triangle_kernel(recv, out, left, right, tri):
    slot = lax.broadcasted_iota(jnp.int32, (8, 128), 1) // 32

    def pick(parts):
        got = parts[0]
        for z in range(1, 4):
            got = jnp.where(slot == z, parts[z], got)
        return got

    def gather(r, _):
        base = pl.multiple_of(48 * r, 16)
        for tile in range(6):
            src = {}
            for z in range(4):
                q, m = divmod(4 * tile + z, 3)
                block = recv[8 * r + q, 24 * m : 24 * (m + 1), :].astype(F32)
                for h in range(3):
                    src[z, h] = block[8 * h : 8 * (h + 1)]
            for at, dest in ((LEFT_AT, left), (RIGHT_AT, right)):
                got = [pick([roll_slots(src[z, h], z - s) for z in range(4)]) for h, s in at]
                for b in range(0, 6, 2):
                    dest[pl.ds(base + 8 * b, 16), 128 * tile : 128 * (tile + 1)] = (
                        jnp.concatenate(got[b : b + 2], axis=0).astype(BF16)
                    )
        return 0

    lax.fori_loop(0, 16, gather, 0)
    for block in range(3):
        rows = slice(256 * block, 256 * (block + 1))
        tri[rows, :] = dot(left[rows, :], right[...], NT)

    def scatter(r, _):
        base = pl.multiple_of(48 * r, 16)
        for q in range(8):
            full, tails = [], []
            for m in range(3):
                tile, z = divmod(3 * q + m, 4)
                cols = slice(128 * tile, 128 * (tile + 1))
                piece = [tri[pl.ds(base + 8 * b, 8), cols] for b in range(6)]
                full.append(pick([roll_slots(piece[b], b - z) for b in range(4)]))
                tail = pick(
                    [roll_slots(piece[4 + s % 2], s - z) for s in range(4)]
                )
                tails.append(jnp.where(slot[:4] < 2, tail[:4], tail[4:]))
            out[8 * r + q] = jnp.concatenate(full + tails, axis=0).astype(BF16)
        return 0

    lax.fori_loop(0, 16, scatter, 0)


def triangle(recv):
    return pl.pallas_call(
        triangle_kernel,
        in_specs=[pl.BlockSpec(memory_space=pltpu.VMEM)],
        out_specs=pl.BlockSpec(memory_space=pltpu.VMEM),
        out_shape=jax.ShapeDtypeStruct((128, 36, 128), BF16),
        scratch_shapes=[
            pltpu.VMEM((768, 768), BF16),
            pltpu.VMEM((768, 768), BF16),
            pltpu.VMEM((768, 768), F32),
        ],
        compiler_params=pltpu.CompilerParams(vmem_limit_bytes=VMEM),
    )(recv)


def update_kernel(
    tri, tri_tail, normed, pair, code, eye, emb, gain, bias, gate_weight, out_weight, out
):
    for col in range(12):
        sums = (tri[col] if col < 8 else tri_tail[col - 8]).astype(F32)
        tri_normed = norm_sublanes(sums, gain[...], bias[...])
        hot = one_hot_rows(code[0, col : col + 1, :])
        turned = dot(eye[...], jnp.concatenate([tri_normed, normed[0, col], hot], axis=0), NT)
        turned = turned.astype(BF16)
        update = dot(turned[:, :128], out_weight[...])
        gate = sigmoid(dot(turned[:, 128:256], gate_weight[...]))
        embedded = dot(turned[:, 256:], emb[...])
        rows = column_rows(col)
        x = jnp.concatenate([pair[i] for i in rows], axis=0).astype(F32)
        result = (x + embedded + gate * update).astype(BF16)
        for s, i in enumerate(rows):
            out[i] = result[32 * s : 32 * (s + 1)]


def update(tri, normed, pair, code, eye, emb, gain, bias, gate_weight, out_weight):
    whole = lambda a: pl.BlockSpec(a.shape, lambda m: (0,) * a.ndim)
    return pl.pallas_call(
        update_kernel,
        grid=(3,),
        in_specs=[
            pl.BlockSpec((8, 128, 128), lambda m: (m, 0, 0)),
            pl.BlockSpec((4, 128, 128), lambda m: (6 + m, 0, 0)),
            pl.BlockSpec((1, 12, 128, 128), lambda m: (m, 0, 0, 0)),
            pl.BlockSpec((48, 32, 128), lambda m: (0, m, 0)),
            pl.BlockSpec((1, 12, 128), lambda m: (m, 0, 0)),
            whole(eye),
            whole(emb),
            whole(gain),
            whole(bias),
            whole(gate_weight),
            whole(out_weight),
        ],
        out_specs=pl.BlockSpec((48, 32, 128), lambda m: (0, m, 0)),
        out_shape=jax.ShapeDtypeStruct((48, 96, 128), BF16),
        compiler_params=pltpu.CompilerParams(vmem_limit_bytes=VMEM),
    )(tri, tri, normed, pair, code, eye, emb, gain, bias, gate_weight, out_weight)


def pair_codes(bins, mask):
    rows, cols = bins.shape
    mask_rows = lax.dynamic_slice_in_dim(mask, lax.axis_index("row") * rows, rows)
    mask_cols = lax.dynamic_slice_in_dim(mask, lax.axis_index("col") * cols, cols)
    code = bins + 16 * mask_rows[:, None] * mask_cols[None, :]
    code = code.reshape(6, 8, 3, 32)
    head = code[:4].transpose(2, 1, 0, 3).reshape(3, 8, 128)
    tail = code[4:].reshape(2, 2, 4, 3, 32).transpose(3, 2, 1, 0, 4).reshape(3, 4, 128)
    return jnp.concatenate([head, tail], axis=1)


def body(
    pair,
    bins,
    mask,
    emb_table,
    ln_gain,
    ln_bias,
    proj_weight,
    gate_weight,
    norm_gain,
    norm_bias,
    out_weight,
):
    code = pair_codes(bins, mask)
    eye = jnp.eye(128, dtype=BF16)
    emb = jnp.pad(emb_table, ((0, 1), (0, 0)))
    column = lambda v: v.reshape(128, 1)
    sides, normed = project(
        pair, code, eye, emb.T, column(ln_gain), column(ln_bias), proj_weight.T
    )
    recv = lax.all_to_all(sides.transpose(1, 0, 2), ("row", "col"), 0, 0, tiled=True)
    sums = lax.all_to_all(triangle(recv), ("row", "col"), 0, 0, tiled=True)
    return update(
        sums.transpose(1, 0, 2),
        normed,
        pair,
        code,
        eye,
        emb,
        column(norm_gain),
        column(norm_bias),
        gate_weight,
        out_weight,
    )


def solution(mesh):
    placed = (P("row", "col", None), P("row", "col"), P(), P(), P(), P(), P(), P(), P(), P(), P())
    return jax.shard_map(
        body, mesh=mesh, in_specs=placed, out_specs=P("row", "col", None), check_vma=False
    )
```

```python
import jax
import jax.numpy as jnp
from jax import lax
from jax.experimental import pallas as pl
from jax.experimental.pallas import tpu as pltpu
from jax.sharding import PartitionSpec as P

EPS = 1e-5
F32 = jnp.float32
BF16 = jnp.bfloat16
I32 = jnp.int32
NT = (((1,), (1,)), ((), ()))
TN = (((0,), (0,)), ((), ()))
NN = (((1,), (0,)), ((), ()))
LIMIT = 24 * 1024 * 1024
IN_HBM = pl.BlockSpec(memory_space=pltpu.HBM)
IN_VMEM = pl.BlockSpec(memory_space=pltpu.VMEM)


def column_row(col, entry):
    if col < 8:
        return 8 * entry + col
    return 32 + 8 * (entry % 2) + 4 * (entry // 2) + col - 8


def lanes_slot(shape):
    return lax.broadcasted_iota(I32, shape, len(shape) - 1) // 32


def pick(entry, parts):
    got = parts[0]
    for e in range(1, 4):
        got = jnp.where(entry == e, parts[e], got)
    return got


def sigmoid(x):
    return 0.5 * jnp.tanh(0.5 * x) + 0.5


def norm_sublanes(x, gain, bias):
    mean = jnp.mean(x, axis=0, keepdims=True)
    centred = x - mean
    var = jnp.mean(centred * centred, axis=0, keepdims=True)
    scaled = centred * lax.rsqrt(var + EPS)
    return [scaled[:, n : n + 128] * gain + bias for n in range(0, x.shape[1], 128)]


def in_hbm(*arrays):
    return [pltpu.with_memory_space_constraint(a, pltpu.HBM) for a in arrays]


def dot(a, b, dims=NN):
    return lax.dot_general(a, b, dims, preferred_element_type=F32)


def down(row):
    return jnp.broadcast_to(row, (128, 128)).T


def eye128():
    rows = lax.broadcasted_iota(I32, (128, 128), 0)
    cols = lax.broadcasted_iota(I32, (128, 128), 1)
    return jnp.where(rows == cols, 1.0, 0.0).astype(BF16)


def padded(emb):
    return jnp.concatenate([emb.astype(F32), jnp.zeros((113, 128), F32)], axis=0)


def columns(codes, shift, rot):
    entry = (lanes_slot((8, 128)) + 4 - rot) % 4
    turn = lambda x, e: pltpu.roll(x, 32 * ((e + shift) % 4), 1)
    head = pick(entry, [turn(codes[8 * b : 8 * b + 8, :], b) for b in range(4)])
    ends = [turn(codes[32 + 8 * (e % 2) : 40 + 8 * (e % 2), :], e) for e in range(4)]
    tail = pick(entry[:4], [ends[0][:4], ends[1][:4], ends[2][4:], ends[3][4:]])
    return [head[c : c + 1, :] for c in range(8)] + [tail[c : c + 1, :] for c in range(4)]


def one_hot(codes):
    level = lax.broadcasted_iota(I32, (128, codes.shape[1]), 0)
    return jnp.where((codes & 15) == level, 1.0, 0.0).astype(BF16)


def half_columns(half):
    return [2 * half, 2 * half + 1, 2 * half + 4, 2 * half + 5, 8 + 2 * half, 9 + 2 * half]


def project_kernel(
    mask_h, pair_h, bins_h, emb_h, gain_h, bias_h, weight_h, out,
    mask, pair, bins, emb, gain, bias, weight, code, normed, done, sems,
):
    r, q = lax.axis_index("row"), lax.axis_index("col")
    small = [
        pltpu.make_async_copy(a, b, sems.at[n])
        for n, (a, b) in enumerate(
            ((mask_h, mask), (weight_h, weight), (gain_h, gain), (bias_h, bias), (emb_h, emb), (bins_h, bins))
        )
    ]
    large = []
    for m in range(3):
        at = (slice(None), pl.ds(32 * m, 32))
        large.append(pltpu.make_async_copy(pair_h.at[at], pair.at[at], sems.at[6 + m]))
    for copy in small + large:
        copy.start()
    for copy in small[:4]:
        copy.wait()

    weight_t = (0.5 * weight[...].astype(F32)).T.astype(BF16)
    gain_t, bias_t = down(gain[...]), down(bias[...])
    lane = lax.broadcasted_iota(I32, (8, 128), 1)
    sub = lax.broadcasted_iota(I32, (8, 128), 0)
    along = [jnp.zeros((8, 128), I32) for _ in range(4)]
    for k in range(96):
        along[k % 4] = jnp.where(lane == k, mask[96 * q + k], along[k % 4])
    along = 16 * (along[0] + along[1] + along[2] + along[3])
    for b in range(6):
        across = jnp.zeros((8, 128), I32)
        for g in range(8):
            across = jnp.where(sub == g, mask[48 * r + 8 * b + g], across)
        code[8 * b : 8 * b + 8, :] = across * along
    for copy in small[4:]:
        copy.wait()
    emb_t = padded(emb[...]).T.astype(BF16)
    code[:, :96] = code[:, :96] + bins[...]
    eye = eye128()
    for copy in large:
        copy.wait()
    for m in range(3):
        rot = (3 * q + m) % 4
        codes = jnp.concatenate(columns(code, 3 * q, rot), axis=1)
        rows = [
            pair[column_row(c, (s + 4 - rot) % 4), 32 * m : 32 * m + 32]
            for c in range(12)
            for s in range(4)
        ]
        x = jnp.concatenate(rows, axis=0)
        summed = dot(eye, x, NT) + dot(emb_t, one_hot(codes))
        parts = jnp.concatenate(norm_sublanes(summed, gain_t, bias_t), axis=1)
        normed[:, 1536 * m : 1536 * (m + 1)] = jnp.where(codes >= 16, parts, 0.0).astype(BF16)

    for m in range(3):
        low = (lanes_slot((128, 128)) + 4 - (3 * q + m) % 4) % 4 < 2
        sides = []
        for side in range(2):
            proj = dot(
                weight_t[256 * side : 256 * (side + 1)], normed[:, 1536 * m : 1536 * (m + 1)]
            )
            value, gate = proj[:128], proj[128:]
            sides.append((jnp.tanh(gate) + 1.0) * value)
        left, right = sides
        for g in range(8):
            own = slice(128 * g, 128 * (g + 1))
            end = slice(128 * (8 + g % 4), 128 * (9 + g % 4))
            left_end, right_end = left[:, end], right[:, end]
            if g < 4:
                left_end = pltpu.roll(left_end, 64, 1)
            else:
                right_end = pltpu.roll(right_end, 64, 1)
            done[24 * m + g] = left[:, own].astype(BF16)
            done[24 * m + 8 + g] = jnp.where(low, right[:, own], left_end).astype(BF16)
            done[24 * m + 16 + g] = jnp.where(low, right_end, right[:, own]).astype(BF16)
    out[...] = jnp.swapaxes(done[...], 0, 1)


def project(mask, pair, bins, emb, gain, bias, weight):
    return pl.pallas_call(
        project_kernel,
        in_specs=[IN_HBM] * 7,
        out_specs=IN_VMEM,
        out_shape=jax.ShapeDtypeStruct((128, 72, 128), BF16),
        scratch_shapes=[
            pltpu.SMEM((768,), I32),
            pltpu.VMEM((48, 96, 128), BF16),
            pltpu.VMEM((48, 96), I32),
            pltpu.VMEM((15, 128), BF16),
            pltpu.VMEM((1, 128), F32),
            pltpu.VMEM((1, 128), F32),
            pltpu.VMEM((128, 512), BF16),
            pltpu.VMEM((48, 128), I32),
            pltpu.VMEM((128, 4608), BF16),
            pltpu.VMEM((72, 128, 128), BF16),
            pltpu.SemaphoreType.DMA((9,)),
        ],
        compiler_params=pltpu.CompilerParams(vmem_limit_bytes=LIMIT),
        name="project",
    )(*in_hbm(mask, pair, bins, emb, gain, bias, weight))


LEFT_AT = [(0, 0), (0, 1), (0, 2), (0, 3), (1, 2), (1, 3)]
RIGHT_AT = [(1, 0), (1, 1), (2, 2), (2, 3), (2, 0), (2, 1)]


def roll_slots(x, by):
    by %= 4
    return x if by == 0 else pltpu.roll(x, 32 * by, 1)


def triangle_kernel(recv, out, left, right, tri, sent, sem):
    slot = lanes_slot((8, 128))

    def gather(r, places, dest):
        for tile in range(6):
            src = []
            for z in range(4):
                q, m = divmod(4 * tile + z, 3)
                src.append(recv[8 * r + q, 24 * m : 24 * (m + 1)].astype(F32))
            got = []
            for h, e in places:
                merged = pick((slot + 4 - e) % 4, [v[8 * h : 8 * (h + 1)] for v in src])
                got.append(roll_slots(merged, -e))
            dest[48 * r : 48 * r + 48, 128 * tile : 128 * (tile + 1)] = (
                jnp.concatenate(got, axis=0).astype(BF16)
            )

    def scatter(r):
        full, ends = {}, {}
        for tile in range(6):
            cols = slice(128 * tile, 128 * (tile + 1))
            piece = [tri[48 * r + 8 * b : 48 * r + 8 * b + 8, cols] for b in range(6)]
            head = [roll_slots(piece[b], b) for b in range(4)]
            tail = [roll_slots(piece[4 + e % 2], e) for e in range(4)]
            tail = [tail[0][:4], tail[1][:4], tail[2][4:], tail[3][4:]]
            for z in range(4):
                entry = (slot + 4 - z) % 4
                full[4 * tile + z] = pick(entry, head)
                ends[4 * tile + z] = pick(entry[:4], tail)
        for q in range(8):
            parts = [full[3 * q + m] for m in range(3)] + [ends[3 * q + m] for m in range(3)]
            sent[8 * r + q] = jnp.concatenate(parts, axis=0).astype(BF16)

    for r in range(16):
        gather(r, RIGHT_AT, right)
        gather(r, LEFT_AT, left)
    tri[...] = dot(left[...], right[...], NT)
    for r in range(16):
        scatter(r)
    copy = pltpu.make_async_copy(sent, out, sem)
    copy.start()
    copy.wait()


def triangle(recv):
    return pl.pallas_call(
        triangle_kernel,
        in_specs=[IN_VMEM],
        out_specs=IN_HBM,
        out_shape=jax.ShapeDtypeStruct((128, 36, 128), BF16),
        scratch_shapes=[
            pltpu.VMEM((768, 768), BF16),
            pltpu.VMEM((768, 768), BF16),
            pltpu.VMEM((768, 768), F32),
            pltpu.VMEM((128, 36, 128), BF16),
            pltpu.SemaphoreType.DMA,
        ],
        compiler_params=pltpu.CompilerParams(vmem_limit_bytes=LIMIT),
        name="triangle",
    )(recv)


def gate_kernel(
    pair, bins, emb, gain, bias, weight, norm_gain, norm_bias, summed_out, gate_out, gain_out, bias_out, code
):
    gain_out[...] = down(norm_gain[...])
    bias_out[...] = down(norm_bias[...])
    gain_t, bias_t = down(gain[...]), down(bias[...])
    emb_rows = padded(emb[...])
    emb_t = emb_rows.T.astype(BF16)
    emb_rows = emb_rows.astype(BF16)
    eye = eye128()
    code[...] = jnp.zeros((48, 128), I32)
    code[:, :96] = bins[...]
    for m in range(3):
        codes_m = columns(code, 4 - m, 0)
        for half in range(2):
            cols = half_columns(half)
            rows = [column_row(c, e) for c in cols for e in range(4)]
            x = jnp.concatenate([pair[i, 32 * m : 32 * m + 32] for i in rows], axis=0)
            hot = one_hot(jnp.concatenate([codes_m[c] for c in cols], axis=1))
            summed = dot(eye, x, NT) + dot(emb_t, hot)
            normed = jnp.concatenate(norm_sublanes(summed, gain_t, bias_t), axis=1).astype(BF16)
            gate = sigmoid(dot(normed, weight[...], TN))
            total = x.astype(F32) + dot(hot, emb_rows, TN)
            for n, i in enumerate(rows):
                summed_out[i, 32 * m : 32 * m + 32] = total[32 * n : 32 * n + 32]
                gate_out[i, 32 * m : 32 * m + 32] = gate[32 * n : 32 * n + 32]


def gates(pair, bins, emb, gain, bias, weight, norm_gain, norm_bias):
    return pl.pallas_call(
        gate_kernel,
        in_specs=[IN_VMEM] * 8,
        out_specs=[IN_VMEM] * 4,
        out_shape=[
            jax.ShapeDtypeStruct((48, 96, 128), F32),
            jax.ShapeDtypeStruct((48, 96, 128), F32),
            jax.ShapeDtypeStruct((128, 128), F32),
            jax.ShapeDtypeStruct((128, 128), F32),
        ],
        scratch_shapes=[pltpu.VMEM((48, 128), I32)],
        compiler_params=pltpu.CompilerParams(vmem_limit_bytes=LIMIT),
        cost_estimate=pl.CostEstimate(flops=10**9, bytes_accessed=10**7, transcendentals=10**6),
        name="gates",
    )(pair, bins, emb, gain, bias, weight, norm_gain, norm_bias)


def update_kernel(
    tri_h, summed_h, gate_h, gain, bias, weight, out, tri, summed, gate, sums, result, sems
):
    load = pltpu.make_async_copy(tri_h, tri, sems.at[3])
    load.start()
    loads = []
    for m in range(3):
        part = (slice(None), pl.ds(32 * m, 32))
        for n, (src, dst) in enumerate(((summed_h, summed), (gate_h, gate))):
            loads.append(pltpu.make_async_copy(src.at[part], dst.at[part], sems.at[4 + 2 * m + n]))
            loads[-1].start()
    q = lax.axis_index("col")
    load.wait()
    sums[...] = jnp.swapaxes(tri[...], 0, 1)
    stores = []
    for m in range(3):
        rot = (3 * q + m) % 4
        at = slice(32 * m, 32 * m + 32)
        loads[2 * m].wait()
        loads[2 * m + 1].wait()
        for first in range(0, 12, 4):
            cols = range(first, first + 4)
            x = [sums[8 * m + c if c < 8 else 16 + 4 * m + c].astype(F32) for c in cols]
            normed = norm_sublanes(jnp.concatenate(x, axis=1), gain[...], bias[...])
            change = dot(jnp.concatenate(normed, axis=1).astype(BF16), weight[...], TN)
            for n, c in enumerate(cols):
                for s in range(4):
                    i = column_row(c, (s + 4 - rot) % 4)
                    k = 128 * n + 32 * s
                    new = summed[i, at] + gate[i, at] * change[k : k + 32]
                    result[i, at] = new.astype(BF16)
        part = (slice(None), pl.ds(32 * m, 32))
        stores.append(pltpu.make_async_copy(result.at[part], out.at[part], sems.at[m]))
        stores[-1].start()
    for store in stores:
        store.wait()


def update(tri, summed, gate, gain, bias, weight):
    return pl.pallas_call(
        update_kernel,
        in_specs=[IN_HBM] * 3 + [IN_VMEM] * 3,
        out_specs=IN_HBM,
        out_shape=jax.ShapeDtypeStruct((48, 96, 128), BF16),
        scratch_shapes=[
            pltpu.VMEM((128, 36, 128), BF16),
            pltpu.VMEM((48, 96, 128), F32),
            pltpu.VMEM((48, 96, 128), F32),
            pltpu.VMEM((36, 128, 128), BF16),
            pltpu.VMEM((48, 96, 128), BF16),
            pltpu.SemaphoreType.DMA((10,)),
        ],
        compiler_params=pltpu.CompilerParams(vmem_limit_bytes=LIMIT),
        name="update",
    )(*in_hbm(tri, summed, gate), gain, bias, weight)


def body(
    pair,
    bins,
    mask,
    emb_table,
    ln_gain,
    ln_bias,
    proj_weight,
    gate_weight,
    norm_gain,
    norm_bias,
    out_weight,
):
    row = lambda v: v.reshape(1, 128)
    sides = project(mask, pair, bins, emb_table, row(ln_gain), row(ln_bias), proj_weight)
    recv = lax.all_to_all(sides, ("row", "col"), 0, 0, tiled=True)
    partial = triangle(recv)
    pair, partial = lax.optimization_barrier((pair, partial))
    summed, gate, gain, bias = gates(
        pair, bins, emb_table, row(ln_gain), row(ln_bias), gate_weight, row(norm_gain), row(norm_bias)
    )
    tri = lax.all_to_all(partial, ("row", "col"), 0, 0, tiled=True)
    return update(tri, summed, gate, gain, bias, out_weight)


def solution(mesh):
    placed = (P("row", "col", None), P("row", "col"), P(), P(), P(), P(), P(), P(), P(), P(), P())
    return jax.shard_map(
        body, mesh=mesh, in_specs=placed, out_specs=P("row", "col", None), check_vma=False
    )
```

```python
import jax
import jax.numpy as jnp
from jax import lax
from jax.experimental import pallas as pl
from jax.experimental.pallas import tpu as pltpu
from jax.sharding import PartitionSpec as P

EPS = 1e-5
F32 = jnp.float32
BF16 = jnp.bfloat16
I32 = jnp.int32
NT = (((1,), (1,)), ((), ()))
TN = (((0,), (0,)), ((), ()))
NN = (((1,), (0,)), ((), ()))
LIMIT = 24 * 1024 * 1024
IN_HBM = pl.BlockSpec(memory_space=pltpu.HBM)
IN_VMEM = pl.BlockSpec(memory_space=pltpu.VMEM)


def column_row(col, entry):
    if col < 8:
        return 8 * entry + col
    return 32 + 8 * (entry % 2) + 4 * (entry // 2) + col - 8


def lanes_slot(shape):
    return lax.broadcasted_iota(I32, shape, len(shape) - 1) // 32


def pick(entry, parts):
    got = parts[0]
    for e in range(1, 4):
        got = jnp.where(entry == e, parts[e], got)
    return got


def sigmoid(x):
    return 0.5 * jnp.tanh(0.5 * x) + 0.5


def norm_sublanes(x, gain, bias):
    mean = jnp.mean(x, axis=0, keepdims=True)
    centred = x - mean
    var = jnp.mean(centred * centred, axis=0, keepdims=True)
    scaled = centred * lax.rsqrt(var + EPS)
    return [scaled[:, n : n + 128] * gain + bias for n in range(0, x.shape[1], 128)]


def in_hbm(*arrays):
    return [pltpu.with_memory_space_constraint(a, pltpu.HBM) for a in arrays]


def dot(a, b, dims=NN):
    return lax.dot_general(a, b, dims, preferred_element_type=F32)


def down(row):
    return jnp.broadcast_to(row, (128, 128)).T


def eye128():
    rows = lax.broadcasted_iota(I32, (128, 128), 0)
    cols = lax.broadcasted_iota(I32, (128, 128), 1)
    return jnp.where(rows == cols, 1.0, 0.0).astype(BF16)


def padded(emb):
    return jnp.concatenate([emb.astype(F32), jnp.zeros((1, 128), F32)], axis=0)


def columns(codes, shift, rot):
    entry = (lanes_slot((8, 128)) + 4 - rot) % 4
    turn = lambda x, e: pltpu.roll(x, 32 * ((e + shift) % 4), 1)
    head = pick(entry, [turn(codes[8 * b : 8 * b + 8, :], b) for b in range(4)])
    ends = [turn(codes[32 + 8 * (e % 2) : 40 + 8 * (e % 2), :], e) for e in range(4)]
    tail = pick(entry[:4], [ends[0][:4], ends[1][:4], ends[2][4:], ends[3][4:]])
    return [head[c : c + 1, :] for c in range(8)] + [tail[c : c + 1, :] for c in range(4)]


def one_hot(codes):
    level = lax.broadcasted_iota(I32, (16, codes.shape[1]), 0)
    return jnp.where((codes & 15) == level, 1.0, 0.0).astype(BF16)


def half_columns(half):
    return [2 * half, 2 * half + 1, 2 * half + 4, 2 * half + 5, 8 + 2 * half, 9 + 2 * half]


def project_kernel(
    mask_h, pair_h, bins_h, emb_h, gain_h, bias_h, weight_h, out, normed_out, codes_out,
    mask, pair, bins, emb, gain, bias, weight, code, normed, done, sems,
):
    r, q = lax.axis_index("row"), lax.axis_index("col")
    small = [
        pltpu.make_async_copy(a, b, sems.at[n])
        for n, (a, b) in enumerate(
            ((mask_h, mask), (weight_h, weight), (gain_h, gain), (bias_h, bias), (emb_h, emb), (bins_h, bins))
        )
    ]
    large = []
    for m in range(3):
        at = (slice(None), pl.ds(32 * m, 32))
        large.append(pltpu.make_async_copy(pair_h.at[at], pair.at[at], sems.at[6 + m]))
    for copy in small + large:
        copy.start()
    for copy in small[:4]:
        copy.wait()

    weight_t = (0.5 * weight[...].astype(F32)).T.astype(BF16)
    gain_t, bias_t = down(gain[...]), down(bias[...])
    lane = lax.broadcasted_iota(I32, (8, 128), 1)
    sub = lax.broadcasted_iota(I32, (8, 128), 0)
    along = [jnp.zeros((8, 128), I32) for _ in range(4)]
    for k in range(96):
        along[k % 4] = jnp.where(lane == k, mask[96 * q + k], along[k % 4])
    along = 16 * (along[0] + along[1] + along[2] + along[3])
    for b in range(6):
        across = jnp.zeros((8, 128), I32)
        for g in range(8):
            across = jnp.where(sub == g, mask[48 * r + 8 * b + g], across)
        code[8 * b : 8 * b + 8, :] = across * along
    for copy in small[4:]:
        copy.wait()
    emb_t = padded(emb[...]).T.astype(BF16)
    code[:, :96] = code[:, :96] + bins[...]
    eye = eye128()
    for copy in large:
        copy.wait()
    for m in range(3):
        rot = (3 * q + m) % 4
        codes = columns(code, 3 * q, rot)
        codes_out[m] = jnp.concatenate(codes, axis=0)
        codes = jnp.concatenate(codes, axis=1)
        rows = [
            pair[column_row(c, (s + 4 - rot) % 4), 32 * m : 32 * m + 32]
            for c in range(12)
            for s in range(4)
        ]
        x = jnp.concatenate(rows, axis=0)
        summed = dot(eye, x, NT) + dot(emb_t, one_hot(codes))
        parts = jnp.concatenate(norm_sublanes(summed, gain_t, bias_t), axis=1)
        normed_out[:, 1536 * m : 1536 * (m + 1)] = parts.astype(BF16)
        normed[:, 1536 * m : 1536 * (m + 1)] = jnp.where(codes >= 16, parts, 0.0).astype(BF16)

    for m in range(3):
        low = (lanes_slot((128, 128)) + 4 - (3 * q + m) % 4) % 4 < 2
        sides = []
        for side in range(2):
            proj = dot(
                weight_t[256 * side : 256 * (side + 1)], normed[:, 1536 * m : 1536 * (m + 1)]
            )
            value, gate = proj[:128], proj[128:]
            sides.append((jnp.tanh(gate) + 1.0) * value)
        left, right = sides
        for g in range(8):
            own = slice(128 * g, 128 * (g + 1))
            end = slice(128 * (8 + g % 4), 128 * (9 + g % 4))
            left_end, right_end = left[:, end], right[:, end]
            if g < 4:
                left_end = pltpu.roll(left_end, 64, 1)
            else:
                right_end = pltpu.roll(right_end, 64, 1)
            done[24 * m + g] = left[:, own].astype(BF16)
            done[24 * m + 8 + g] = jnp.where(low, right[:, own], left_end).astype(BF16)
            done[24 * m + 16 + g] = jnp.where(low, right_end, right[:, own]).astype(BF16)
    out[...] = jnp.swapaxes(done[...], 0, 1)


def project(mask, pair, bins, emb, gain, bias, weight):
    return pl.pallas_call(
        project_kernel,
        in_specs=[IN_HBM] * 7,
        out_specs=[IN_VMEM] * 3,
        out_shape=[
            jax.ShapeDtypeStruct((128, 72, 128), BF16),
            jax.ShapeDtypeStruct((128, 4608), BF16),
            jax.ShapeDtypeStruct((3, 12, 128), I32),
        ],
        scratch_shapes=[
            pltpu.SMEM((768,), I32),
            pltpu.VMEM((48, 96, 128), BF16),
            pltpu.VMEM((48, 96), I32),
            pltpu.VMEM((15, 128), BF16),
            pltpu.VMEM((1, 128), F32),
            pltpu.VMEM((1, 128), F32),
            pltpu.VMEM((128, 512), BF16),
            pltpu.VMEM((48, 128), I32),
            pltpu.VMEM((128, 4608), BF16),
            pltpu.VMEM((72, 128, 128), BF16),
            pltpu.SemaphoreType.DMA((9,)),
        ],
        compiler_params=pltpu.CompilerParams(vmem_limit_bytes=LIMIT),
        name="project",
    )(*in_hbm(mask, pair, bins, emb, gain, bias, weight))


LEFT_AT = [(0, 0), (0, 1), (0, 2), (0, 3), (1, 2), (1, 3)]
RIGHT_AT = [(1, 0), (1, 1), (2, 2), (2, 3), (2, 0), (2, 1)]


def roll_slots(x, by):
    by %= 4
    return x if by == 0 else pltpu.roll(x, 32 * by, 1)


def triangle_kernel(recv, out, left, right, tri):
    slot = lanes_slot((8, 128))

    def gather(r, places, dest):
        for tile in range(6):
            src = []
            for z in range(4):
                q, m = divmod(4 * tile + z, 3)
                src.append(recv[8 * r + q, 24 * m : 24 * (m + 1)].astype(F32))
            got = []
            for h, e in places:
                merged = pick((slot + 4 - e) % 4, [v[8 * h : 8 * (h + 1)] for v in src])
                got.append(roll_slots(merged, -e))
            dest[48 * r : 48 * r + 48, 128 * tile : 128 * (tile + 1)] = (
                jnp.concatenate(got, axis=0).astype(BF16)
            )

    def scatter(r):
        full, ends = {}, {}
        for tile in range(6):
            cols = slice(128 * tile, 128 * (tile + 1))
            piece = [tri[48 * r + 8 * b : 48 * r + 8 * b + 8, cols] for b in range(6)]
            head = [roll_slots(piece[b], b) for b in range(4)]
            tail = [roll_slots(piece[4 + e % 2], e) for e in range(4)]
            tail = [tail[0][:4], tail[1][:4], tail[2][4:], tail[3][4:]]
            for z in range(4):
                entry = (slot + 4 - z) % 4
                full[4 * tile + z] = pick(entry, head)
                ends[4 * tile + z] = pick(entry[:4], tail)
        for q in range(8):
            heads = [full[3 * q + m] for m in range(3)]
            parts = [v[at : at + 4] for v in heads for at in (0, 4)]
            parts += [ends[3 * q + m] for m in range(3)]
            out[8 * r + q] = jnp.concatenate(parts, axis=1).astype(BF16)

    for r in range(16):
        gather(r, RIGHT_AT, right)
        gather(r, LEFT_AT, left)
    tri[...] = dot(left[...], right[...], NT)
    for r in range(16):
        scatter(r)


def triangle(recv):
    return pl.pallas_call(
        triangle_kernel,
        in_specs=[IN_VMEM],
        out_specs=IN_VMEM,
        out_shape=jax.ShapeDtypeStruct((128, 4, 1152), BF16),
        scratch_shapes=[
            pltpu.VMEM((768, 768), BF16),
            pltpu.VMEM((768, 768), BF16),
            pltpu.VMEM((768, 768), F32),
        ],
        compiler_params=pltpu.CompilerParams(vmem_limit_bytes=LIMIT),
        name="triangle",
    )(recv)


def update_kernel(
    tri, normed, codes, pair, emb, gain, bias, gate_weight, out_weight, out, sums, result, sems
):
    q = lax.axis_index("col")
    gain_t, bias_t = down(gain[...]), down(bias[...])
    zeros = jnp.zeros((128, 128), BF16)
    both = jnp.concatenate(
        [
            jnp.concatenate([(0.5 * gate_weight[...].astype(F32)).astype(BF16), zeros], axis=1),
            jnp.concatenate([zeros[:16], padded(emb[...]).astype(BF16)], axis=1),
        ],
        axis=0,
    )
    for u in range(9):
        part = tri[:, :, 128 * u : 128 * (u + 1)].astype(F32)
        sums[4 * u : 4 * u + 4] = jnp.swapaxes(part, 0, 1).astype(BF16)
    stores = []
    for m in range(3):
        rot = (3 * q + m) % 4
        at = slice(32 * m, 32 * m + 32)
        hot = one_hot(jnp.concatenate([codes[m, c : c + 1, :] for c in range(12)], axis=1))
        lanes = slice(1536 * m, 1536 * (m + 1))
        mixed = dot(jnp.concatenate([normed[:, lanes], hot], axis=0), both, TN)
        x = [sums[8 * m + c if c < 8 else 16 + 4 * m + c].astype(F32) for c in range(12)]
        tri_normed = norm_sublanes(jnp.concatenate(x, axis=1), gain_t, bias_t)
        change = dot(jnp.concatenate(tri_normed, axis=1).astype(BF16), out_weight[...], TN)
        change = (0.5 * jnp.tanh(mixed[:, :128]) + 0.5) * change
        for c in range(12):
            for s in range(4):
                i = column_row(c, (s + 4 - rot) % 4)
                k = slice(128 * c + 32 * s, 128 * c + 32 * s + 32)
                total = pair[i, at].astype(F32) + mixed[k, 128:]
                result[i, at] = (total + change[k]).astype(BF16)
        part = (slice(None), pl.ds(32 * m, 32))
        stores.append(pltpu.make_async_copy(result.at[part], out.at[part], sems.at[m]))
        stores[m].start()
    for store in stores:
        store.wait()


def update(*args):
    return pl.pallas_call(
        update_kernel,
        in_specs=[IN_VMEM] * 9,
        out_specs=IN_HBM,
        out_shape=jax.ShapeDtypeStruct((48, 96, 128), BF16),
        scratch_shapes=[
            pltpu.VMEM((36, 128, 128), BF16),
            pltpu.VMEM((48, 96, 128), BF16),
            pltpu.SemaphoreType.DMA((3,)),
        ],
        compiler_params=pltpu.CompilerParams(vmem_limit_bytes=LIMIT),
        name="update",
    )(*args)


def body(
    pair,
    bins,
    mask,
    emb_table,
    ln_gain,
    ln_bias,
    proj_weight,
    gate_weight,
    norm_gain,
    norm_bias,
    out_weight,
):
    row = lambda v: v.reshape(1, 128)
    sides, normed, codes = project(
        mask, pair, bins, emb_table, row(ln_gain), row(ln_bias), proj_weight
    )
    recv = lax.all_to_all(sides, ("row", "col"), 0, 0, tiled=True)
    tri = lax.all_to_all(triangle(recv), ("row", "col"), 0, 0, tiled=True)
    return update(
        tri, normed, codes, pair, emb_table, row(norm_gain), row(norm_bias), gate_weight, out_weight
    )


def solution(mesh):
    placed = (P("row", "col", None), P("row", "col"), P(), P(), P(), P(), P(), P(), P(), P(), P())
    return jax.shard_map(
        body, mesh=mesh, in_specs=placed, out_specs=P("row", "col", None), check_vma=False
    )
```

```python
import jax
import jax.numpy as jnp
from jax import lax
from jax.experimental import pallas as pl
from jax.experimental.pallas import tpu as pltpu
from jax.sharding import PartitionSpec as P

EPS = 1e-5
F32 = jnp.float32
BF16 = jnp.bfloat16
I32 = jnp.int32
NT = (((1,), (1,)), ((), ()))
TN = (((0,), (0,)), ((), ()))
NN = (((1,), (0,)), ((), ()))
LIMIT = 24 * 1024 * 1024
IN_HBM = pl.BlockSpec(memory_space=pltpu.HBM)
IN_VMEM = pl.BlockSpec(memory_space=pltpu.VMEM)


def column_row(col, entry):
    if col < 8:
        return 8 * entry + col
    return 32 + 8 * (entry % 2) + 4 * (entry // 2) + col - 8


def lanes_slot(shape):
    return lax.broadcasted_iota(I32, shape, len(shape) - 1) // 32


def pick(entry, parts):
    got = parts[0]
    for e in range(1, 4):
        got = jnp.where(entry == e, parts[e], got)
    return got


def sigmoid(x):
    return 0.5 * jnp.tanh(0.5 * x) + 0.5


def norm_sublanes(x, gain, bias):
    mean = jnp.mean(x, axis=0, keepdims=True)
    centred = x - mean
    var = jnp.mean(centred * centred, axis=0, keepdims=True)
    scaled = centred * lax.rsqrt(var + EPS)
    return [scaled[:, n : n + 128] * gain + bias for n in range(0, x.shape[1], 128)]


def in_hbm(*arrays):
    return [pltpu.with_memory_space_constraint(a, pltpu.HBM) for a in arrays]


def dot(a, b, dims=NN):
    return lax.dot_general(a, b, dims, preferred_element_type=F32)


def down(row):
    return jnp.broadcast_to(row, (128, 128)).T


def eye128():
    rows = lax.broadcasted_iota(I32, (128, 128), 0)
    cols = lax.broadcasted_iota(I32, (128, 128), 1)
    return jnp.where(rows == cols, 1.0, 0.0).astype(BF16)


def padded(emb):
    return jnp.concatenate([emb.astype(F32), jnp.zeros((1, 128), F32)], axis=0)


def columns(codes, shift, rot):
    entry = (lanes_slot((8, 128)) + 4 - rot) % 4
    turn = lambda x, e: pltpu.roll(x, 32 * ((e + shift) % 4), 1)
    head = pick(entry, [turn(codes[8 * b : 8 * b + 8, :], b) for b in range(4)])
    ends = [turn(codes[32 + 8 * (e % 2) : 40 + 8 * (e % 2), :], e) for e in range(4)]
    tail = pick(entry[:4], [ends[0][:4], ends[1][:4], ends[2][4:], ends[3][4:]])
    return [head[c : c + 1, :] for c in range(8)] + [tail[c : c + 1, :] for c in range(4)]


def one_hot(codes):
    level = lax.broadcasted_iota(I32, (16, codes.shape[1]), 0)
    return jnp.where((codes & 15) == level, 1.0, 0.0).astype(BF16)


def half_columns(half):
    return [2 * half, 2 * half + 1, 2 * half + 4, 2 * half + 5, 8 + 2 * half, 9 + 2 * half]


def project_kernel(
    mask_h, pair_h, bins_h, emb_h, gain_h, bias_h, weight_h, out, normed_out, codes_out,
    mask, pair, bins, emb, gain, bias, weight, code, normed, done, sems,
):
    r, q = lax.axis_index("row"), lax.axis_index("col")
    small = [
        pltpu.make_async_copy(a, b, sems.at[n])
        for n, (a, b) in enumerate(
            ((mask_h, mask), (weight_h, weight), (gain_h, gain), (bias_h, bias), (emb_h, emb), (bins_h, bins))
        )
    ]
    large = []
    for m in range(3):
        at = (slice(None), pl.ds(32 * m, 32))
        large.append(pltpu.make_async_copy(pair_h.at[at], pair.at[at], sems.at[6 + m]))
    for copy in small + large:
        copy.start()
    for copy in small[:4]:
        copy.wait()

    weight_t = (0.5 * weight[...].astype(F32)).T.astype(BF16)
    gain_t, bias_t = down(gain[...]), down(bias[...])
    lane = lax.broadcasted_iota(I32, (8, 128), 1)
    sub = lax.broadcasted_iota(I32, (8, 128), 0)
    along = [jnp.zeros((8, 128), I32) for _ in range(4)]
    for k in range(96):
        along[k % 4] = jnp.where(lane == k, mask[96 * q + k], along[k % 4])
    along = 16 * (along[0] + along[1] + along[2] + along[3])
    for b in range(6):
        across = jnp.zeros((8, 128), I32)
        for g in range(8):
            across = jnp.where(sub == g, mask[48 * r + 8 * b + g], across)
        code[8 * b : 8 * b + 8, :] = across * along
    for copy in small[4:]:
        copy.wait()
    emb_t = padded(emb[...]).T.astype(BF16)
    code[:, :96] = code[:, :96] + bins[...]
    eye = eye128()
    for copy in large:
        copy.wait()
    for m in range(3):
        rot = (3 * q + m) % 4
        codes = columns(code, 3 * q, rot)
        codes_out[m] = jnp.concatenate(codes, axis=0)
        codes = jnp.concatenate(codes, axis=1)
        rows = [
            pair[column_row(c, (s + 4 - rot) % 4), 32 * m : 32 * m + 32]
            for c in range(12)
            for s in range(4)
        ]
        x = jnp.concatenate(rows, axis=0)
        summed = dot(eye, x, NT) + dot(emb_t, one_hot(codes))
        parts = jnp.concatenate(norm_sublanes(summed, gain_t, bias_t), axis=1)
        normed_out[:, 1536 * m : 1536 * (m + 1)] = parts.astype(BF16)
        normed[:, 1536 * m : 1536 * (m + 1)] = jnp.where(codes >= 16, parts, 0.0).astype(BF16)

    for m in range(3):
        low = (lanes_slot((128, 128)) + 4 - (3 * q + m) % 4) % 4 < 2
        sides = []
        for side in range(2):
            proj = dot(
                weight_t[256 * side : 256 * (side + 1)], normed[:, 1536 * m : 1536 * (m + 1)]
            )
            value, gate = proj[:128], proj[128:]
            sides.append((jnp.tanh(gate) + 1.0) * value)
        left, right = sides
        for g in range(8):
            own = slice(128 * g, 128 * (g + 1))
            end = slice(128 * (8 + g % 4), 128 * (9 + g % 4))
            left_end, right_end = left[:, end], right[:, end]
            if g < 4:
                left_end = pltpu.roll(left_end, 64, 1)
            else:
                right_end = pltpu.roll(right_end, 64, 1)
            done[24 * m + g] = left[:, own].astype(BF16)
            done[24 * m + 8 + g] = jnp.where(low, right[:, own], left_end).astype(BF16)
            done[24 * m + 16 + g] = jnp.where(low, right_end, right[:, own]).astype(BF16)
    out[...] = jnp.swapaxes(done[...], 0, 1)


def project(mask, pair, bins, emb, gain, bias, weight):
    return pl.pallas_call(
        project_kernel,
        in_specs=[IN_HBM] * 7,
        out_specs=[IN_VMEM] * 3,
        out_shape=[
            jax.ShapeDtypeStruct((128, 72, 128), BF16),
            jax.ShapeDtypeStruct((128, 4608), BF16),
            jax.ShapeDtypeStruct((3, 12, 128), I32),
        ],
        scratch_shapes=[
            pltpu.SMEM((768,), I32),
            pltpu.VMEM((48, 96, 128), BF16),
            pltpu.VMEM((48, 96), I32),
            pltpu.VMEM((15, 128), BF16),
            pltpu.VMEM((1, 128), F32),
            pltpu.VMEM((1, 128), F32),
            pltpu.VMEM((128, 512), BF16),
            pltpu.VMEM((48, 128), I32),
            pltpu.VMEM((128, 4608), BF16),
            pltpu.VMEM((72, 128, 128), BF16),
            pltpu.SemaphoreType.DMA((9,)),
        ],
        compiler_params=pltpu.CompilerParams(vmem_limit_bytes=LIMIT),
        name="project",
    )(*in_hbm(mask, pair, bins, emb, gain, bias, weight))


LEFT_AT = [(0, 0), (0, 1), (0, 2), (0, 3), (1, 2), (1, 3)]
RIGHT_AT = [(1, 0), (1, 1), (2, 2), (2, 3), (2, 0), (2, 1)]


def roll_slots(x, by):
    by %= 4
    return x if by == 0 else pltpu.roll(x, 32 * by, 1)


def triangle_kernel(recv, out, left, right, tri):
    slot = lanes_slot((8, 128))

    def gather(r, places, dest):
        for tile in range(6):
            src = []
            for z in range(4):
                q, m = divmod(4 * tile + z, 3)
                src.append(recv[8 * r + q, 24 * m : 24 * (m + 1)].astype(F32))
            got = []
            for h, e in places:
                merged = pick((slot + 4 - e) % 4, [v[8 * h : 8 * (h + 1)] for v in src])
                got.append(roll_slots(merged, -e))
            dest[48 * r : 48 * r + 48, 128 * tile : 128 * (tile + 1)] = (
                jnp.concatenate(got, axis=0).astype(BF16)
            )

    def scatter(r):
        full, ends = {}, {}
        for tile in range(6):
            cols = slice(128 * tile, 128 * (tile + 1))
            piece = [tri[48 * r + 8 * b : 48 * r + 8 * b + 8, cols] for b in range(6)]
            head = [roll_slots(piece[b], b) for b in range(4)]
            tail = [roll_slots(piece[4 + e % 2], e) for e in range(4)]
            tail = [tail[0][:4], tail[1][:4], tail[2][4:], tail[3][4:]]
            for z in range(4):
                entry = (slot + 4 - z) % 4
                full[4 * tile + z] = pick(entry, head)
                ends[4 * tile + z] = pick(entry[:4], tail)
        for q in range(8):
            heads = [full[3 * q + m] for m in range(3)]
            parts = [v[at : at + 4] for v in heads for at in (0, 4)]
            parts += [ends[3 * q + m] for m in range(3)]
            out[8 * r + q] = jnp.concatenate(parts, axis=1).astype(BF16)

    for r in range(16):
        gather(r, RIGHT_AT, right)
        gather(r, LEFT_AT, left)
    tri[...] = dot(left[...], right[...], NT)
    for r in range(16):
        scatter(r)


def triangle(recv):
    return pl.pallas_call(
        triangle_kernel,
        in_specs=[IN_VMEM],
        out_specs=IN_VMEM,
        out_shape=jax.ShapeDtypeStruct((128, 4, 1152), BF16),
        scratch_shapes=[
            pltpu.VMEM((768, 768), BF16),
            pltpu.VMEM((768, 768), BF16),
            pltpu.VMEM((768, 768), F32),
        ],
        compiler_params=pltpu.CompilerParams(vmem_limit_bytes=LIMIT),
        name="triangle",
    )(recv)


def update_kernel(
    tri, normed, codes, pair, emb, gain, bias, gate_weight, out_weight, out, sums, result, sems
):
    q = lax.axis_index("col")
    gain_t, bias_t = down(gain[...]), down(bias[...])
    zeros = jnp.zeros((128, 128), BF16)
    both = jnp.concatenate(
        [
            jnp.concatenate([(0.5 * gate_weight[...].astype(F32)).astype(BF16), zeros], axis=1),
            jnp.concatenate([zeros[:16], padded(emb[...]).astype(BF16)], axis=1),
        ],
        axis=0,
    )
    for u in range(9):
        part = tri[:, :, 128 * u : 128 * (u + 1)].astype(F32)
        sums[512 * u : 512 * (u + 1)] = part.reshape(512, 128)
    stores = []
    for m in range(3):
        rot = (3 * q + m) % 4
        at = slice(32 * m, 32 * m + 32)
        hot = one_hot(jnp.concatenate([codes[m, c : c + 1, :] for c in range(12)], axis=1))
        lanes = slice(1536 * m, 1536 * (m + 1))
        mixed = dot(jnp.concatenate([normed[:, lanes], hot], axis=0), both, TN)
        x = []
        for c in range(12):
            u, v = divmod(8 * m + c if c < 8 else 16 + 4 * m + c, 4)
            x.append(sums[pl.ds(512 * u + v, 128, stride=4), :])
        tri_normed = norm_sublanes(jnp.concatenate(x, axis=1), gain_t, bias_t)
        change = dot(jnp.concatenate(tri_normed, axis=1).astype(BF16), out_weight[...], TN)
        change = (0.5 * jnp.tanh(mixed[:, :128]) + 0.5) * change
        for c in range(12):
            for s in range(4):
                i = column_row(c, (s + 4 - rot) % 4)
                k = slice(128 * c + 32 * s, 128 * c + 32 * s + 32)
                total = pair[i, at].astype(F32) + mixed[k, 128:]
                result[i, at] = (total + change[k]).astype(BF16)
        part = (slice(None), pl.ds(32 * m, 32))
        stores.append(pltpu.make_async_copy(result.at[part], out.at[part], sems.at[m]))
        stores[m].start()
    for store in stores:
        store.wait()


def update(*args):
    return pl.pallas_call(
        update_kernel,
        in_specs=[IN_VMEM] * 9,
        out_specs=IN_HBM,
        out_shape=jax.ShapeDtypeStruct((48, 96, 128), BF16),
        scratch_shapes=[
            pltpu.VMEM((4608, 128), F32),
            pltpu.VMEM((48, 96, 128), BF16),
            pltpu.SemaphoreType.DMA((3,)),
        ],
        compiler_params=pltpu.CompilerParams(vmem_limit_bytes=LIMIT),
        name="update",
    )(*args)


def body(
    pair,
    bins,
    mask,
    emb_table,
    ln_gain,
    ln_bias,
    proj_weight,
    gate_weight,
    norm_gain,
    norm_bias,
    out_weight,
):
    row = lambda v: v.reshape(1, 128)
    sides, normed, codes = project(
        mask, pair, bins, emb_table, row(ln_gain), row(ln_bias), proj_weight
    )
    recv = lax.all_to_all(sides, ("row", "col"), 0, 0, tiled=True)
    tri = lax.all_to_all(triangle(recv), ("row", "col"), 0, 0, tiled=True)
    return update(
        tri, normed, codes, pair, emb_table, row(norm_gain), row(norm_bias), gate_weight, out_weight
    )


def solution(mesh):
    placed = (P("row", "col", None), P("row", "col"), P(), P(), P(), P(), P(), P(), P(), P(), P())
    return jax.shard_map(
        body, mesh=mesh, in_specs=placed, out_specs=P("row", "col", None), check_vma=False
    )
```

```python
import jax
import jax.numpy as jnp
from jax import lax
from jax.experimental import pallas as pl
from jax.experimental.pallas import tpu as pltpu
from jax.sharding import PartitionSpec as P

EPS = 1e-5
F32 = jnp.float32
BF16 = jnp.bfloat16
I32 = jnp.int32
NT = (((1,), (1,)), ((), ()))
TN = (((0,), (0,)), ((), ()))
NN = (((1,), (0,)), ((), ()))
LIMIT = 24 * 1024 * 1024
IN_HBM = pl.BlockSpec(memory_space=pltpu.HBM)
IN_VMEM = pl.BlockSpec(memory_space=pltpu.VMEM)


def column_row(col, entry):
    if col < 8:
        return 8 * entry + col
    return 32 + 8 * (entry % 2) + 4 * (entry // 2) + col - 8


def lanes_slot(shape):
    return lax.broadcasted_iota(I32, shape, len(shape) - 1) // 32


def pick(entry, parts):
    got = parts[0]
    for e in range(1, 4):
        got = jnp.where(entry == e, parts[e], got)
    return got


def sigmoid(x):
    return 0.5 * jnp.tanh(0.5 * x) + 0.5


def norm_sublanes(x, gain, bias):
    mean = jnp.mean(x, axis=0, keepdims=True)
    centred = x - mean
    var = jnp.mean(centred * centred, axis=0, keepdims=True)
    scaled = centred * lax.rsqrt(var + EPS)
    return [scaled[:, n : n + 128] * gain + bias for n in range(0, x.shape[1], 128)]


def in_hbm(*arrays):
    return [pltpu.with_memory_space_constraint(a, pltpu.HBM) for a in arrays]


def dot(a, b, dims=NN):
    return lax.dot_general(a, b, dims, preferred_element_type=F32)


def down(row):
    return jnp.broadcast_to(row, (128, 128)).T


def eye128():
    rows = lax.broadcasted_iota(I32, (128, 128), 0)
    cols = lax.broadcasted_iota(I32, (128, 128), 1)
    return jnp.where(rows == cols, 1.0, 0.0).astype(BF16)


def padded(emb):
    return jnp.concatenate([emb.astype(F32), jnp.zeros((1, 128), F32)], axis=0)


def columns(codes, shift, rot):
    entry = (lanes_slot((8, 128)) + 4 - rot) % 4
    turn = lambda x, e: pltpu.roll(x, 32 * ((e + shift) % 4), 1)
    head = pick(entry, [turn(codes[8 * b : 8 * b + 8, :], b) for b in range(4)])
    ends = [turn(codes[32 + 8 * (e % 2) : 40 + 8 * (e % 2), :], e) for e in range(4)]
    tail = pick(entry[:4], [ends[0][:4], ends[1][:4], ends[2][4:], ends[3][4:]])
    return [head[c : c + 1, :] for c in range(8)] + [tail[c : c + 1, :] for c in range(4)]


def one_hot(codes):
    level = lax.broadcasted_iota(I32, (16, codes.shape[1]), 0)
    return jnp.where((codes & 15) == level, 1.0, 0.0).astype(BF16)


def half_columns(half):
    return [2 * half, 2 * half + 1, 2 * half + 4, 2 * half + 5, 8 + 2 * half, 9 + 2 * half]


def project_kernel(
    mask_h, pair_h, bins_h, emb_h, gain_h, bias_h, weight_h, out, normed_out, codes_out,
    mask, pair, bins, emb, gain, bias, weight, code, normed, done, sems,
):
    r, q = lax.axis_index("row"), lax.axis_index("col")
    small = [
        pltpu.make_async_copy(a, b, sems.at[n])
        for n, (a, b) in enumerate(
            ((mask_h, mask), (weight_h, weight), (gain_h, gain), (bias_h, bias), (emb_h, emb), (bins_h, bins))
        )
    ]
    large = []
    for m in range(3):
        at = (slice(None), pl.ds(32 * m, 32))
        large.append(pltpu.make_async_copy(pair_h.at[at], pair.at[at], sems.at[6 + m]))
    for copy in small + large:
        copy.start()
    for copy in small[:4]:
        copy.wait()

    weight_t = (0.5 * weight[...].astype(F32)).T.astype(BF16)
    gain_t, bias_t = down(gain[...]), down(bias[...])
    lane = lax.broadcasted_iota(I32, (8, 128), 1)
    sub = lax.broadcasted_iota(I32, (8, 128), 0)
    along = [jnp.zeros((8, 128), I32) for _ in range(4)]
    for k in range(96):
        along[k % 4] = jnp.where(lane == k, mask[96 * q + k], along[k % 4])
    along = 16 * (along[0] + along[1] + along[2] + along[3])
    for b in range(6):
        across = jnp.zeros((8, 128), I32)
        for g in range(8):
            across = jnp.where(sub == g, mask[48 * r + 8 * b + g], across)
        code[8 * b : 8 * b + 8, :] = across * along
    for copy in small[4:]:
        copy.wait()
    emb_t = padded(emb[...]).T.astype(BF16)
    code[:, :96] = code[:, :96] + bins[...]
    eye = eye128()
    for copy in large:
        copy.wait()
    for m in range(3):
        rot = (3 * q + m) % 4
        codes = columns(code, 3 * q, rot)
        codes_out[m] = jnp.concatenate(codes, axis=0)
        codes = jnp.concatenate(codes, axis=1)
        rows = [
            pair[column_row(c, (s + 4 - rot) % 4), 32 * m : 32 * m + 32]
            for c in range(12)
            for s in range(4)
        ]
        x = jnp.concatenate(rows, axis=0)
        summed = dot(eye, x, NT) + dot(emb_t, one_hot(codes))
        parts = jnp.concatenate(norm_sublanes(summed, gain_t, bias_t), axis=1)
        normed_out[:, 1536 * m : 1536 * (m + 1)] = parts.astype(BF16)
        normed[:, 1536 * m : 1536 * (m + 1)] = jnp.where(codes >= 16, parts, 0.0).astype(BF16)

    for m in range(3):
        low = (lanes_slot((128, 128)) + 4 - (3 * q + m) % 4) % 4 < 2
        sides = []
        for side in range(2):
            proj = dot(
                weight_t[256 * side : 256 * (side + 1)], normed[:, 1536 * m : 1536 * (m + 1)]
            )
            value, gate = proj[:128], proj[128:]
            sides.append((jnp.tanh(gate) + 1.0) * value)
        left, right = sides
        for g in range(8):
            own = slice(128 * g, 128 * (g + 1))
            end = slice(128 * (8 + g % 4), 128 * (9 + g % 4))
            left_end, right_end = left[:, end], right[:, end]
            if g < 4:
                left_end = pltpu.roll(left_end, 64, 1)
            else:
                right_end = pltpu.roll(right_end, 64, 1)
            done[24 * m + g] = left[:, own].astype(BF16)
            done[24 * m + 8 + g] = jnp.where(low, right[:, own], left_end).astype(BF16)
            done[24 * m + 16 + g] = jnp.where(low, right_end, right[:, own]).astype(BF16)
    out[...] = jnp.swapaxes(done[...], 0, 1)


def project(mask, pair, bins, emb, gain, bias, weight):
    return pl.pallas_call(
        project_kernel,
        in_specs=[IN_HBM] * 7,
        out_specs=[IN_VMEM] * 3,
        out_shape=[
            jax.ShapeDtypeStruct((128, 72, 128), BF16),
            jax.ShapeDtypeStruct((128, 4608), BF16),
            jax.ShapeDtypeStruct((3, 12, 128), I32),
        ],
        scratch_shapes=[
            pltpu.SMEM((768,), I32),
            pltpu.VMEM((48, 96, 128), BF16),
            pltpu.VMEM((48, 96), I32),
            pltpu.VMEM((15, 128), BF16),
            pltpu.VMEM((1, 128), F32),
            pltpu.VMEM((1, 128), F32),
            pltpu.VMEM((128, 512), BF16),
            pltpu.VMEM((48, 128), I32),
            pltpu.VMEM((128, 4608), BF16),
            pltpu.VMEM((72, 128, 128), BF16),
            pltpu.SemaphoreType.DMA((9,)),
        ],
        compiler_params=pltpu.CompilerParams(vmem_limit_bytes=LIMIT),
        name="project",
    )(*in_hbm(mask, pair, bins, emb, gain, bias, weight))


LEFT_AT = [(0, 0), (0, 1), (0, 2), (0, 3), (1, 2), (1, 3)]
RIGHT_AT = [(1, 0), (1, 1), (2, 2), (2, 3), (2, 0), (2, 1)]


def roll_slots(x, by):
    by %= 4
    return x if by == 0 else pltpu.roll(x, 32 * by, 1)


def triangle_kernel(recv, out, left, right, tri):
    slot = lanes_slot((8, 128))

    def gather(r, places, dest):
        for tile in range(6):
            src = []
            for z in range(4):
                q, m = divmod(4 * tile + z, 3)
                src.append(recv[16 * q + r, 24 * m : 24 * (m + 1)].astype(F32))
            got = []
            for h, e in places:
                merged = pick((slot + 4 - e) % 4, [v[8 * h : 8 * (h + 1)] for v in src])
                got.append(roll_slots(merged, -e))
            dest[48 * r : 48 * r + 48, 128 * tile : 128 * (tile + 1)] = (
                jnp.concatenate(got, axis=0).astype(BF16)
            )

    def scatter(r):
        full, ends = {}, {}
        for tile in range(6):
            cols = slice(128 * tile, 128 * (tile + 1))
            piece = [tri[48 * r + 8 * b : 48 * r + 8 * b + 8, cols] for b in range(6)]
            head = [roll_slots(piece[b], b) for b in range(4)]
            tail = [roll_slots(piece[4 + e % 2], e) for e in range(4)]
            tail = [tail[0][:4], tail[1][:4], tail[2][4:], tail[3][4:]]
            for z in range(4):
                entry = (slot + 4 - z) % 4
                full[4 * tile + z] = pick(entry, head)
                ends[4 * tile + z] = pick(entry[:4], tail)
        for q in range(8):
            heads = [full[3 * q + m] for m in range(3)]
            parts = [v[at : at + 4] for v in heads for at in (0, 4)]
            parts += [ends[3 * q + m] for m in range(3)]
            out[16 * q + r] = jnp.concatenate(parts, axis=1).astype(BF16)

    for r in range(16):
        gather(r, RIGHT_AT, right)
        gather(r, LEFT_AT, left)
    tri[...] = dot(left[...], right[...], NT)
    for r in range(16):
        scatter(r)


def triangle(recv):
    return pl.pallas_call(
        triangle_kernel,
        in_specs=[IN_VMEM],
        out_specs=IN_VMEM,
        out_shape=jax.ShapeDtypeStruct((128, 4, 1152), BF16),
        scratch_shapes=[
            pltpu.VMEM((768, 768), BF16),
            pltpu.VMEM((768, 768), BF16),
            pltpu.VMEM((768, 768), F32),
        ],
        compiler_params=pltpu.CompilerParams(vmem_limit_bytes=LIMIT),
        name="triangle",
    )(recv)


def update_kernel(
    tri, normed, codes, pair, emb, gain, bias, gate_weight, out_weight, out, sums, result, sems
):
    q = lax.axis_index("col")
    gain_t, bias_t = down(gain[...]), down(bias[...])
    zeros = jnp.zeros((128, 128), BF16)
    both = jnp.concatenate(
        [
            jnp.concatenate([(0.5 * gate_weight[...].astype(F32)).astype(BF16), zeros], axis=1),
            jnp.concatenate([zeros[:16], padded(emb[...]).astype(BF16)], axis=1),
        ],
        axis=0,
    )
    for u in range(9):
        part = tri[:, :, 128 * u : 128 * (u + 1)].astype(F32)
        sums[512 * u : 512 * (u + 1)] = part.reshape(512, 128)
    stores = []
    for m in range(3):
        rot = (3 * q + m) % 4
        at = slice(32 * m, 32 * m + 32)
        hot = one_hot(jnp.concatenate([codes[m, c : c + 1, :] for c in range(12)], axis=1))
        lanes = slice(1536 * m, 1536 * (m + 1))
        mixed = dot(jnp.concatenate([normed[:, lanes], hot], axis=0), both, TN)
        x = []
        for c in range(12):
            u, v = divmod(8 * m + c if c < 8 else 16 + 4 * m + c, 4)
            x.append(sums[pl.ds(512 * u + v, 128, stride=4), :])
        tri_normed = norm_sublanes(jnp.concatenate(x, axis=1), gain_t, bias_t)
        change = dot(jnp.concatenate(tri_normed, axis=1).astype(BF16), out_weight[...], TN)
        change = (0.5 * jnp.tanh(mixed[:, :128]) + 0.5) * change
        for c in range(12):
            for s in range(4):
                i = column_row(c, (s + 4 - rot) % 4)
                k = slice(128 * c + 32 * s, 128 * c + 32 * s + 32)
                total = pair[i, at].astype(F32) + mixed[k, 128:]
                result[i, at] = (total + change[k]).astype(BF16)
        part = (slice(None), pl.ds(32 * m, 32))
        stores.append(pltpu.make_async_copy(result.at[part], out.at[part], sems.at[m]))
        stores[m].start()
    for store in stores:
        store.wait()


def update(*args):
    return pl.pallas_call(
        update_kernel,
        in_specs=[IN_VMEM] * 9,
        out_specs=IN_HBM,
        out_shape=jax.ShapeDtypeStruct((48, 96, 128), BF16),
        scratch_shapes=[
            pltpu.VMEM((4608, 128), F32),
            pltpu.VMEM((48, 96, 128), BF16),
            pltpu.SemaphoreType.DMA((3,)),
        ],
        compiler_params=pltpu.CompilerParams(vmem_limit_bytes=LIMIT),
        name="update",
    )(*args)


def body(
    pair,
    bins,
    mask,
    emb_table,
    ln_gain,
    ln_bias,
    proj_weight,
    gate_weight,
    norm_gain,
    norm_bias,
    out_weight,
):
    row = lambda v: v.reshape(1, 128)
    sides, normed, codes = project(
        mask, pair, bins, emb_table, row(ln_gain), row(ln_bias), proj_weight
    )
    recv = lax.all_to_all(sides, ("col", "row"), 0, 0, tiled=True)
    tri = lax.all_to_all(triangle(recv), ("col", "row"), 0, 0, tiled=True)
    return update(
        tri, normed, codes, pair, emb_table, row(norm_gain), row(norm_bias), gate_weight, out_weight
    )


def solution(mesh):
    placed = (P("row", "col", None), P("row", "col"), P(), P(), P(), P(), P(), P(), P(), P(), P())
    return jax.shard_map(
        body, mesh=mesh, in_specs=placed, out_specs=P("row", "col", None), check_vma=False
    )
```

```python
import jax
import jax.numpy as jnp
from jax import lax
from jax.experimental import pallas as pl
from jax.experimental.pallas import tpu as pltpu
from jax.sharding import PartitionSpec as P

EPS = 1e-5
F32 = jnp.float32
BF16 = jnp.bfloat16
I32 = jnp.int32
NT = (((1,), (1,)), ((), ()))
TN = (((0,), (0,)), ((), ()))
NN = (((1,), (0,)), ((), ()))
LIMIT = 24 * 1024 * 1024
IN_HBM = pl.BlockSpec(memory_space=pltpu.HBM)
IN_VMEM = pl.BlockSpec(memory_space=pltpu.VMEM)


def column_row(col, entry):
    if col < 8:
        return 8 * entry + col
    return 32 + 8 * (entry % 2) + 4 * (entry // 2) + col - 8


def lanes_slot(shape):
    return lax.broadcasted_iota(I32, shape, len(shape) - 1) // 32


def pick(entry, parts):
    got = parts[0]
    for e in range(1, 4):
        got = jnp.where(entry == e, parts[e], got)
    return got


def sigmoid(x):
    return 0.5 * jnp.tanh(0.5 * x) + 0.5


def norm_sublanes(x, gain, bias):
    mean = jnp.mean(x, axis=0, keepdims=True)
    centred = x - mean
    var = jnp.mean(centred * centred, axis=0, keepdims=True)
    scaled = centred * lax.rsqrt(var + EPS)
    return [scaled[:, n : n + 128] * gain + bias for n in range(0, x.shape[1], 128)]


def in_hbm(*arrays):
    return [pltpu.with_memory_space_constraint(a, pltpu.HBM) for a in arrays]


def dot(a, b, dims=NN):
    return lax.dot_general(a, b, dims, preferred_element_type=F32)


def down(row):
    return jnp.broadcast_to(row, (128, 128)).T


def eye128():
    rows = lax.broadcasted_iota(I32, (128, 128), 0)
    cols = lax.broadcasted_iota(I32, (128, 128), 1)
    return jnp.where(rows == cols, 1.0, 0.0).astype(BF16)


def padded(emb):
    return jnp.concatenate([emb.astype(F32), jnp.zeros((1, 128), F32)], axis=0)


def gate_weights(gate_weight, emb):
    zeros = jnp.zeros((128, 128), BF16)
    gate = jnp.concatenate([(0.5 * gate_weight.astype(F32)).astype(BF16), zeros], axis=1)
    return jnp.concatenate(
        [gate, jnp.concatenate([zeros[:16], padded(emb).astype(BF16)], axis=1)], axis=0
    )


def gate_and_total(m, rot, normed, codes, pair, weights):
    hot = one_hot(jnp.concatenate([codes[m, c : c + 1, :] for c in range(12)], axis=1))
    lanes = slice(1536 * m, 1536 * (m + 1))
    mixed = dot(jnp.concatenate([normed[:, lanes], hot], axis=0), weights, TN)
    rows = [
        pair[column_row(c, (s + 4 - rot) % 4), 32 * m : 32 * m + 32]
        for c in range(12)
        for s in range(4)
    ]
    gate = 0.5 * jnp.tanh(mixed[:, :128]) + 0.5
    return gate, jnp.concatenate(rows, axis=0).astype(F32) + mixed[:, 128:]


def ahead(q):
    return q % 2 == 0


def columns(codes, shift, rot):
    entry = (lanes_slot((8, 128)) + 4 - rot) % 4
    turn = lambda x, e: pltpu.roll(x, 32 * ((e + shift) % 4), 1)
    head = pick(entry, [turn(codes[8 * b : 8 * b + 8, :], b) for b in range(4)])
    ends = [turn(codes[32 + 8 * (e % 2) : 40 + 8 * (e % 2), :], e) for e in range(4)]
    tail = pick(entry[:4], [ends[0][:4], ends[1][:4], ends[2][4:], ends[3][4:]])
    return [head[c : c + 1, :] for c in range(8)] + [tail[c : c + 1, :] for c in range(4)]


def one_hot(codes):
    level = lax.broadcasted_iota(I32, (16, codes.shape[1]), 0)
    return jnp.where((codes & 15) == level, 1.0, 0.0).astype(BF16)


def half_columns(half):
    return [2 * half, 2 * half + 1, 2 * half + 4, 2 * half + 5, 8 + 2 * half, 9 + 2 * half]


def project_kernel(
    mask_h, pair_h, bins_h, emb_h, gain_h, bias_h, weight_h, gate_weight_h,
    out, normed_out, codes_out, gate_out, total_out,
    mask, pair, bins, emb, gain, bias, weight, gate_weight, code, normed, done, sems,
):
    r, q = lax.axis_index("row"), lax.axis_index("col")
    small = [
        pltpu.make_async_copy(a, b, sems.at[n])
        for n, (a, b) in enumerate(
            ((mask_h, mask), (weight_h, weight), (gain_h, gain), (bias_h, bias), (emb_h, emb), (bins_h, bins), (gate_weight_h, gate_weight))
        )
    ]
    large = []
    for m in range(3):
        at = (slice(None), pl.ds(32 * m, 32))
        large.append(pltpu.make_async_copy(pair_h.at[at], pair.at[at], sems.at[7 + m]))
    for copy in small + large:
        copy.start()
    for copy in small[:4]:
        copy.wait()

    weight_t = (0.5 * weight[...].astype(F32)).T.astype(BF16)
    gain_t, bias_t = down(gain[...]), down(bias[...])
    lane = lax.broadcasted_iota(I32, (8, 128), 1)
    sub = lax.broadcasted_iota(I32, (8, 128), 0)
    along = [jnp.zeros((8, 128), I32) for _ in range(4)]
    for k in range(96):
        along[k % 4] = jnp.where(lane == k, mask[96 * q + k], along[k % 4])
    along = 16 * (along[0] + along[1] + along[2] + along[3])
    for b in range(6):
        across = jnp.zeros((8, 128), I32)
        for g in range(8):
            across = jnp.where(sub == g, mask[48 * r + 8 * b + g], across)
        code[8 * b : 8 * b + 8, :] = across * along
    for copy in small[4:]:
        copy.wait()
    emb_t = padded(emb[...]).T.astype(BF16)
    code[:, :96] = code[:, :96] + bins[...]
    eye = eye128()
    for copy in large:
        copy.wait()
    for m in range(3):
        rot = (3 * q + m) % 4
        codes = columns(code, 3 * q, rot)
        codes_out[m] = jnp.concatenate(codes, axis=0)
        codes = jnp.concatenate(codes, axis=1)
        rows = [
            pair[column_row(c, (s + 4 - rot) % 4), 32 * m : 32 * m + 32]
            for c in range(12)
            for s in range(4)
        ]
        x = jnp.concatenate(rows, axis=0)
        summed = dot(eye, x, NT) + dot(emb_t, one_hot(codes))
        parts = jnp.concatenate(norm_sublanes(summed, gain_t, bias_t), axis=1)
        normed_out[:, 1536 * m : 1536 * (m + 1)] = parts.astype(BF16)
        normed[:, 1536 * m : 1536 * (m + 1)] = jnp.where(codes >= 16, parts, 0.0).astype(BF16)

    for m in range(3):
        low = (lanes_slot((128, 128)) + 4 - (3 * q + m) % 4) % 4 < 2
        sides = []
        for side in range(2):
            proj = dot(
                weight_t[256 * side : 256 * (side + 1)], normed[:, 1536 * m : 1536 * (m + 1)]
            )
            value, gate = proj[:128], proj[128:]
            sides.append((jnp.tanh(gate) + 1.0) * value)
        left, right = sides
        for g in range(8):
            own = slice(128 * g, 128 * (g + 1))
            end = slice(128 * (8 + g % 4), 128 * (9 + g % 4))
            left_end, right_end = left[:, end], right[:, end]
            if g < 4:
                left_end = pltpu.roll(left_end, 64, 1)
            else:
                right_end = pltpu.roll(right_end, 64, 1)
            done[24 * m + g] = left[:, own].astype(BF16)
            done[24 * m + 8 + g] = jnp.where(low, right[:, own], left_end).astype(BF16)
            done[24 * m + 16 + g] = jnp.where(low, right_end, right[:, own]).astype(BF16)
    out[...] = jnp.swapaxes(done[...], 0, 1)

    @pl.when(ahead(q))
    def _():
        weights = gate_weights(gate_weight[...], emb[...])
        for m in range(3):
            lanes = slice(1536 * m, 1536 * (m + 1))
            gate_out[lanes], total_out[lanes] = gate_and_total(
                m, (3 * q + m) % 4, normed_out, codes_out, pair, weights
            )


def project(*args):
    return pl.pallas_call(
        project_kernel,
        in_specs=[IN_HBM] * 8,
        out_specs=[IN_VMEM] * 5,
        out_shape=[
            jax.ShapeDtypeStruct((128, 72, 128), BF16),
            jax.ShapeDtypeStruct((128, 4608), BF16),
            jax.ShapeDtypeStruct((3, 12, 128), I32),
            jax.ShapeDtypeStruct((4608, 128), F32),
            jax.ShapeDtypeStruct((4608, 128), F32),
        ],
        scratch_shapes=[
            pltpu.SMEM((768,), I32),
            pltpu.VMEM((48, 96, 128), BF16),
            pltpu.VMEM((48, 96), I32),
            pltpu.VMEM((15, 128), BF16),
            pltpu.VMEM((1, 128), F32),
            pltpu.VMEM((1, 128), F32),
            pltpu.VMEM((128, 512), BF16),
            pltpu.VMEM((128, 128), BF16),
            pltpu.VMEM((48, 128), I32),
            pltpu.VMEM((128, 4608), BF16),
            pltpu.VMEM((72, 128, 128), BF16),
            pltpu.SemaphoreType.DMA((10,)),
        ],
        compiler_params=pltpu.CompilerParams(vmem_limit_bytes=LIMIT),
        name="project",
    )(*in_hbm(*args))


LEFT_AT = [(0, 0), (0, 1), (0, 2), (0, 3), (1, 2), (1, 3)]
RIGHT_AT = [(1, 0), (1, 1), (2, 2), (2, 3), (2, 0), (2, 1)]


def roll_slots(x, by):
    by %= 4
    return x if by == 0 else pltpu.roll(x, 32 * by, 1)


def triangle_kernel(recv, out, left, right, tri):
    slot = lanes_slot((8, 128))

    def gather(r, places, dest):
        for tile in range(6):
            src = []
            for z in range(4):
                q, m = divmod(4 * tile + z, 3)
                src.append(recv[16 * q + r, 24 * m : 24 * (m + 1)].astype(F32))
            got = []
            for h, e in places:
                merged = pick((slot + 4 - e) % 4, [v[8 * h : 8 * (h + 1)] for v in src])
                got.append(roll_slots(merged, -e))
            dest[48 * r : 48 * r + 48, 128 * tile : 128 * (tile + 1)] = (
                jnp.concatenate(got, axis=0).astype(BF16)
            )

    def scatter(r):
        full, ends = {}, {}
        for tile in range(6):
            cols = slice(128 * tile, 128 * (tile + 1))
            piece = [tri[48 * r + 8 * b : 48 * r + 8 * b + 8, cols] for b in range(6)]
            head = [roll_slots(piece[b], b) for b in range(4)]
            tail = [roll_slots(piece[4 + e % 2], e) for e in range(4)]
            tail = [tail[0][:4], tail[1][:4], tail[2][4:], tail[3][4:]]
            for z in range(4):
                entry = (slot + 4 - z) % 4
                full[4 * tile + z] = pick(entry, head)
                ends[4 * tile + z] = pick(entry[:4], tail)
        for q in range(8):
            heads = [full[3 * q + m] for m in range(3)]
            parts = [v[at : at + 4] for v in heads for at in (0, 4)]
            parts += [ends[3 * q + m] for m in range(3)]
            out[16 * q + r] = jnp.concatenate(parts, axis=1).astype(BF16)

    for r in range(16):
        gather(r, RIGHT_AT, right)
        gather(r, LEFT_AT, left)
    tri[...] = dot(left[...], right[...], NT)
    for r in range(16):
        scatter(r)


def triangle(recv):
    return pl.pallas_call(
        triangle_kernel,
        in_specs=[IN_VMEM],
        out_specs=IN_VMEM,
        out_shape=jax.ShapeDtypeStruct((128, 4, 1152), BF16),
        scratch_shapes=[
            pltpu.VMEM((768, 768), BF16),
            pltpu.VMEM((768, 768), BF16),
            pltpu.VMEM((768, 768), F32),
        ],
        compiler_params=pltpu.CompilerParams(vmem_limit_bytes=LIMIT),
        name="triangle",
    )(recv)


def update_kernel(
    tri, normed, codes, gate_in, total_in, pair, emb, gain, bias, gate_weight, out_weight, out,
    sums, result, sems,
):
    q = lax.axis_index("col")
    stores = [
        pltpu.make_async_copy(result.at[part], out.at[part], sems.at[m])
        for m, part in enumerate([(slice(None), pl.ds(32 * m, 32)) for m in range(3)])
    ]

    def finish(gates):
        gain_t, bias_t = down(gain[...]), down(bias[...])
        for u in range(9):
            part = tri[:, :, 128 * u : 128 * (u + 1)].astype(F32)
            sums[512 * u : 512 * (u + 1)] = part.reshape(512, 128)
        for m in range(3):
            rot = (3 * q + m) % 4
            gate, total = gates(m, rot)
            x = []
            for c in range(12):
                u, v = divmod(8 * m + c if c < 8 else 16 + 4 * m + c, 4)
                x.append(sums[pl.ds(512 * u + v, 128, stride=4), :])
            tri_normed = norm_sublanes(jnp.concatenate(x, axis=1), gain_t, bias_t)
            tri_normed = jnp.concatenate(tri_normed, axis=1).astype(BF16)
            new = total + gate * dot(tri_normed, out_weight[...], TN)
            for c in range(12):
                for s in range(4):
                    k = 128 * c + 32 * s
                    i = column_row(c, (s + 4 - rot) % 4)
                    result[i, 32 * m : 32 * m + 32] = new[k : k + 32].astype(BF16)
            stores[m].start()

    @pl.when(ahead(q))
    def _():
        def gates(m, rot):
            lanes = slice(1536 * m, 1536 * (m + 1))
            return gate_in[lanes], total_in[lanes]

        finish(gates)

    @pl.when(jnp.logical_not(ahead(q)))
    def _():
        weights = gate_weights(gate_weight[...], emb[...])
        finish(lambda m, rot: gate_and_total(m, rot, normed, codes, pair, weights))

    for store in stores:
        store.wait()


def update(*args):
    return pl.pallas_call(
        update_kernel,
        in_specs=[IN_VMEM] * 11,
        out_specs=IN_HBM,
        out_shape=jax.ShapeDtypeStruct((48, 96, 128), BF16),
        scratch_shapes=[
            pltpu.VMEM((4608, 128), F32),
            pltpu.VMEM((48, 96, 128), BF16),
            pltpu.SemaphoreType.DMA((3,)),
        ],
        compiler_params=pltpu.CompilerParams(vmem_limit_bytes=LIMIT),
        name="update",
    )(*args)


def body(
    pair,
    bins,
    mask,
    emb_table,
    ln_gain,
    ln_bias,
    proj_weight,
    gate_weight,
    norm_gain,
    norm_bias,
    out_weight,
):
    row = lambda v: v.reshape(1, 128)
    sides, *kept = project(
        mask, pair, bins, emb_table, row(ln_gain), row(ln_bias), proj_weight, gate_weight
    )
    recv = lax.all_to_all(sides, ("col", "row"), 0, 0, tiled=True)
    tri = lax.all_to_all(triangle(recv), ("col", "row"), 0, 0, tiled=True)
    return update(
        tri, *kept, pair, emb_table, row(norm_gain), row(norm_bias), gate_weight, out_weight
    )


def solution(mesh):
    placed = (P("row", "col", None), P("row", "col"), P(), P(), P(), P(), P(), P(), P(), P(), P())
    return jax.shard_map(
        body, mesh=mesh, in_specs=placed, out_specs=P("row", "col", None), check_vma=False
    )
```

```python
import jax
import jax.numpy as jnp
from jax import lax
from jax.experimental import pallas as pl
from jax.experimental.pallas import tpu as pltpu
from jax.sharding import PartitionSpec as P

EPS = 1e-5
F32 = jnp.float32
BF16 = jnp.bfloat16
I32 = jnp.int32
NT = (((1,), (1,)), ((), ()))
TN = (((0,), (0,)), ((), ()))
NN = (((1,), (0,)), ((), ()))
ROW, COL = ("y", "z_lo", "core"), ("x", "z_hi")
CORE_FIRST = ("core", "y", "z_lo", "x", "z_hi")
LIMIT = 24 * 1024 * 1024
IN_HBM = pl.BlockSpec(memory_space=pltpu.HBM)
IN_VMEM = pl.BlockSpec(memory_space=pltpu.VMEM)


def column_row(col, entry):
    if col < 8:
        return 8 * entry + col
    return 32 + 8 * (entry % 2) + 4 * (entry // 2) + col - 8


def lanes_slot(shape):
    return lax.broadcasted_iota(I32, shape, len(shape) - 1) // 32


def pick(entry, parts):
    got = parts[0]
    for e in range(1, 4):
        got = jnp.where(entry == e, parts[e], got)
    return got


def sigmoid(x):
    return 0.5 * jnp.tanh(0.5 * x) + 0.5


def norm_sublanes(x, gain, bias):
    mean = jnp.mean(x, axis=0, keepdims=True)
    centred = x - mean
    var = jnp.mean(centred * centred, axis=0, keepdims=True)
    scaled = centred * lax.rsqrt(var + EPS)
    return [scaled[:, n : n + 128] * gain + bias for n in range(0, x.shape[1], 128)]


def in_hbm(*arrays):
    return [pltpu.with_memory_space_constraint(a, pltpu.HBM) for a in arrays]


def dot(a, b, dims=NN):
    return lax.dot_general(a, b, dims, preferred_element_type=F32)


def down(row):
    return jnp.broadcast_to(row, (128, 128)).T


def eye128():
    rows = lax.broadcasted_iota(I32, (128, 128), 0)
    cols = lax.broadcasted_iota(I32, (128, 128), 1)
    return jnp.where(rows == cols, 1.0, 0.0).astype(BF16)


def padded(emb):
    return jnp.concatenate([emb.astype(F32), jnp.zeros((1, 128), F32)], axis=0)


def gate_weights(gate_weight, emb):
    zeros = jnp.zeros((128, 128), BF16)
    gate = jnp.concatenate([(0.5 * gate_weight.astype(F32)).astype(BF16), zeros], axis=1)
    return jnp.concatenate(
        [gate, jnp.concatenate([zeros[:16], padded(emb).astype(BF16)], axis=1)], axis=0
    )


def gate_and_total(m, rot, normed, codes, pair, weights):
    hot = one_hot(jnp.concatenate([codes[m, c : c + 1, :] for c in range(12)], axis=1))
    lanes = slice(1536 * m, 1536 * (m + 1))
    mixed = dot(jnp.concatenate([normed[:, lanes], hot], axis=0), weights, TN)
    rows = [
        pair[column_row(c, (s + 4 - rot) % 4), 32 * m : 32 * m + 32]
        for c in range(12)
        for s in range(4)
    ]
    gate = 0.5 * jnp.tanh(mixed[:, :128]) + 0.5
    return gate, jnp.concatenate(rows, axis=0).astype(F32) + mixed[:, 128:]


def place_row():
    return 4 * lax.axis_index("y") + 2 * lax.axis_index("z_lo") + lax.axis_index("core")


def place_col():
    return 2 * lax.axis_index("x") + lax.axis_index("z_hi")


def ahead(q):
    return q % 2 == 0


def columns(codes, shift, rot):
    entry = (lanes_slot((8, 128)) + 4 - rot) % 4
    turn = lambda x, e: pltpu.roll(x, 32 * ((e + shift) % 4), 1)
    head = pick(entry, [turn(codes[8 * b : 8 * b + 8, :], b) for b in range(4)])
    ends = [turn(codes[32 + 8 * (e % 2) : 40 + 8 * (e % 2), :], e) for e in range(4)]
    tail = pick(entry[:4], [ends[0][:4], ends[1][:4], ends[2][4:], ends[3][4:]])
    return [head[c : c + 1, :] for c in range(8)] + [tail[c : c + 1, :] for c in range(4)]


def one_hot(codes):
    level = lax.broadcasted_iota(I32, (16, codes.shape[1]), 0)
    return jnp.where((codes & 15) == level, 1.0, 0.0).astype(BF16)


def half_columns(half):
    return [2 * half, 2 * half + 1, 2 * half + 4, 2 * half + 5, 8 + 2 * half, 9 + 2 * half]


def project_kernel(
    mask_h, pair_h, bins_h, emb_h, gain_h, bias_h, weight_h, gate_weight_h,
    out, normed_out, codes_out, gate_out, total_out,
    mask, pair, bins, emb, gain, bias, weight, gate_weight, code, normed, done, sems,
):
    r, q = place_row(), place_col()
    small = [
        pltpu.make_async_copy(a, b, sems.at[n])
        for n, (a, b) in enumerate(
            ((mask_h, mask), (weight_h, weight), (gain_h, gain), (bias_h, bias), (emb_h, emb), (bins_h, bins), (gate_weight_h, gate_weight))
        )
    ]
    large = []
    for m in range(3):
        at = (slice(None), pl.ds(32 * m, 32))
        large.append(pltpu.make_async_copy(pair_h.at[at], pair.at[at], sems.at[7 + m]))
    for copy in small + large:
        copy.start()
    for copy in small[:4]:
        copy.wait()

    weight_t = (0.5 * weight[...].astype(F32)).T.astype(BF16)
    gain_t, bias_t = down(gain[...]), down(bias[...])
    lane = lax.broadcasted_iota(I32, (8, 128), 1)
    sub = lax.broadcasted_iota(I32, (8, 128), 0)
    along = [jnp.zeros((8, 128), I32) for _ in range(4)]
    for k in range(96):
        along[k % 4] = jnp.where(lane == k, mask[96 * q + k], along[k % 4])
    along = 16 * (along[0] + along[1] + along[2] + along[3])
    for b in range(6):
        across = jnp.zeros((8, 128), I32)
        for g in range(8):
            across = jnp.where(sub == g, mask[48 * r + 8 * b + g], across)
        code[8 * b : 8 * b + 8, :] = across * along
    for copy in small[4:]:
        copy.wait()
    emb_t = padded(emb[...]).T.astype(BF16)
    code[:, :96] = code[:, :96] + bins[...]
    eye = eye128()
    for copy in large:
        copy.wait()
    for m in range(3):
        rot = (3 * q + m) % 4
        codes = columns(code, 3 * q, rot)
        codes_out[m] = jnp.concatenate(codes, axis=0)
        codes = jnp.concatenate(codes, axis=1)
        rows = [
            pair[column_row(c, (s + 4 - rot) % 4), 32 * m : 32 * m + 32]
            for c in range(12)
            for s in range(4)
        ]
        x = jnp.concatenate(rows, axis=0)
        summed = dot(eye, x, NT) + dot(emb_t, one_hot(codes))
        parts = jnp.concatenate(norm_sublanes(summed, gain_t, bias_t), axis=1)
        normed_out[:, 1536 * m : 1536 * (m + 1)] = parts.astype(BF16)
        normed[:, 1536 * m : 1536 * (m + 1)] = jnp.where(codes >= 16, parts, 0.0).astype(BF16)

    for m in range(3):
        low = (lanes_slot((128, 128)) + 4 - (3 * q + m) % 4) % 4 < 2
        sides = []
        for side in range(2):
            proj = dot(
                weight_t[256 * side : 256 * (side + 1)], normed[:, 1536 * m : 1536 * (m + 1)]
            )
            value, gate = proj[:128], proj[128:]
            sides.append((jnp.tanh(gate) + 1.0) * value)
        left, right = sides
        for g in range(8):
            own = slice(128 * g, 128 * (g + 1))
            end = slice(128 * (8 + g % 4), 128 * (9 + g % 4))
            left_end, right_end = left[:, end], right[:, end]
            if g < 4:
                left_end = pltpu.roll(left_end, 64, 1)
            else:
                right_end = pltpu.roll(right_end, 64, 1)
            done[24 * m + g] = left[:, own].astype(BF16)
            done[24 * m + 8 + g] = jnp.where(low, right[:, own], left_end).astype(BF16)
            done[24 * m + 16 + g] = jnp.where(low, right_end, right[:, own]).astype(BF16)
    out[...] = jnp.swapaxes(done[...], 0, 1)

    @pl.when(ahead(q))
    def _():
        weights = gate_weights(gate_weight[...], emb[...])
        for m in range(3):
            lanes = slice(1536 * m, 1536 * (m + 1))
            gate_out[lanes], total_out[lanes] = gate_and_total(
                m, (3 * q + m) % 4, normed_out, codes_out, pair, weights
            )


def project(*args):
    return pl.pallas_call(
        project_kernel,
        in_specs=[IN_HBM] * 8,
        out_specs=[IN_VMEM] * 5,
        out_shape=[
            jax.ShapeDtypeStruct((128, 72, 128), BF16),
            jax.ShapeDtypeStruct((128, 4608), BF16),
            jax.ShapeDtypeStruct((3, 12, 128), I32),
            jax.ShapeDtypeStruct((4608, 128), F32),
            jax.ShapeDtypeStruct((4608, 128), F32),
        ],
        scratch_shapes=[
            pltpu.SMEM((768,), I32),
            pltpu.VMEM((48, 96, 128), BF16),
            pltpu.VMEM((48, 96), I32),
            pltpu.VMEM((15, 128), BF16),
            pltpu.VMEM((1, 128), F32),
            pltpu.VMEM((1, 128), F32),
            pltpu.VMEM((128, 512), BF16),
            pltpu.VMEM((128, 128), BF16),
            pltpu.VMEM((48, 128), I32),
            pltpu.VMEM((128, 4608), BF16),
            pltpu.VMEM((72, 128, 128), BF16),
            pltpu.SemaphoreType.DMA((10,)),
        ],
        compiler_params=pltpu.CompilerParams(vmem_limit_bytes=LIMIT),
        name="project",
    )(*in_hbm(*args))


LEFT_AT = [(0, 0), (0, 1), (0, 2), (0, 3), (1, 2), (1, 3)]
RIGHT_AT = [(1, 0), (1, 1), (2, 2), (2, 3), (2, 0), (2, 1)]


def roll_slots(x, by):
    by %= 4
    return x if by == 0 else pltpu.roll(x, 32 * by, 1)


def triangle_kernel(recv, out, left, right, tri):
    slot = lanes_slot((8, 128))

    def gather(r, places, dest):
        for tile in range(6):
            src = []
            for z in range(4):
                q, m = divmod(4 * tile + z, 3)
                src.append(recv[64 * (r % 2) + 8 * (r // 2) + q, 24 * m : 24 * (m + 1)].astype(F32))
            got = []
            for h, e in places:
                merged = pick((slot + 4 - e) % 4, [v[8 * h : 8 * (h + 1)] for v in src])
                got.append(roll_slots(merged, -e))
            dest[48 * r : 48 * r + 48, 128 * tile : 128 * (tile + 1)] = (
                jnp.concatenate(got, axis=0).astype(BF16)
            )

    def scatter(r):
        full, ends = {}, {}
        for tile in range(6):
            cols = slice(128 * tile, 128 * (tile + 1))
            piece = [tri[48 * r + 8 * b : 48 * r + 8 * b + 8, cols] for b in range(6)]
            head = [roll_slots(piece[b], b) for b in range(4)]
            tail = [roll_slots(piece[4 + e % 2], e) for e in range(4)]
            tail = [tail[0][:4], tail[1][:4], tail[2][4:], tail[3][4:]]
            for z in range(4):
                entry = (slot + 4 - z) % 4
                full[4 * tile + z] = pick(entry, head)
                ends[4 * tile + z] = pick(entry[:4], tail)
        for q in range(8):
            heads = [full[3 * q + m] for m in range(3)]
            parts = [v[at : at + 4] for v in heads for at in (0, 4)]
            parts += [ends[3 * q + m] for m in range(3)]
            out[64 * (r % 2) + 8 * (r // 2) + q] = jnp.concatenate(parts, axis=1).astype(BF16)

    for r in range(16):
        gather(r, RIGHT_AT, right)
        gather(r, LEFT_AT, left)
    tri[...] = dot(left[...], right[...], NT)
    for r in range(16):
        scatter(r)


def triangle(recv):
    return pl.pallas_call(
        triangle_kernel,
        in_specs=[IN_VMEM],
        out_specs=IN_VMEM,
        out_shape=jax.ShapeDtypeStruct((128, 4, 1152), BF16),
        scratch_shapes=[
            pltpu.VMEM((768, 768), BF16),
            pltpu.VMEM((768, 768), BF16),
            pltpu.VMEM((768, 768), F32),
        ],
        compiler_params=pltpu.CompilerParams(vmem_limit_bytes=LIMIT),
        name="triangle",
    )(recv)


def update_kernel(
    tri, normed, codes, gate_in, total_in, pair, emb, gain, bias, gate_weight, out_weight, out,
    sums, result, sems,
):
    q = place_col()
    stores = [
        pltpu.make_async_copy(result.at[part], out.at[part], sems.at[m])
        for m, part in enumerate([(slice(None), pl.ds(32 * m, 32)) for m in range(3)])
    ]

    def finish(gates):
        gain_t, bias_t = down(gain[...]), down(bias[...])
        for u in range(9):
            part = tri[:, :, 128 * u : 128 * (u + 1)].astype(F32)
            sums[512 * u : 512 * (u + 1)] = part.reshape(512, 128)
        for m in range(3):
            rot = (3 * q + m) % 4
            gate, total = gates(m, rot)
            x = []
            for c in range(12):
                u, v = divmod(8 * m + c if c < 8 else 16 + 4 * m + c, 4)
                x.append(sums[pl.ds(512 * u + v, 128, stride=4), :])
            tri_normed = norm_sublanes(jnp.concatenate(x, axis=1), gain_t, bias_t)
            tri_normed = jnp.concatenate(tri_normed, axis=1).astype(BF16)
            new = total + gate * dot(tri_normed, out_weight[...], TN)
            for c in range(12):
                for s in range(4):
                    k = 128 * c + 32 * s
                    i = column_row(c, (s + 4 - rot) % 4)
                    result[i, 32 * m : 32 * m + 32] = new[k : k + 32].astype(BF16)
            stores[m].start()

    @pl.when(ahead(q))
    def _():
        def gates(m, rot):
            lanes = slice(1536 * m, 1536 * (m + 1))
            return gate_in[lanes], total_in[lanes]

        finish(gates)

    @pl.when(jnp.logical_not(ahead(q)))
    def _():
        weights = gate_weights(gate_weight[...], emb[...])
        finish(lambda m, rot: gate_and_total(m, rot, normed, codes, pair, weights))

    for store in stores:
        store.wait()


def update(*args):
    return pl.pallas_call(
        update_kernel,
        in_specs=[IN_VMEM] * 11,
        out_specs=IN_HBM,
        out_shape=jax.ShapeDtypeStruct((48, 96, 128), BF16),
        scratch_shapes=[
            pltpu.VMEM((4608, 128), F32),
            pltpu.VMEM((48, 96, 128), BF16),
            pltpu.SemaphoreType.DMA((3,)),
        ],
        compiler_params=pltpu.CompilerParams(vmem_limit_bytes=LIMIT),
        name="update",
    )(*args)


def body(
    pair,
    bins,
    mask,
    emb_table,
    ln_gain,
    ln_bias,
    proj_weight,
    gate_weight,
    norm_gain,
    norm_bias,
    out_weight,
):
    row = lambda v: v.reshape(1, 128)
    sides, *kept = project(
        mask, pair, bins, emb_table, row(ln_gain), row(ln_bias), proj_weight, gate_weight
    )
    recv = lax.all_to_all(sides, CORE_FIRST, 0, 0, tiled=True)
    tri = lax.all_to_all(triangle(recv), CORE_FIRST, 0, 0, tiled=True)
    return update(
        tri, *kept, pair, emb_table, row(norm_gain), row(norm_bias), gate_weight, out_weight
    )


def solution(mesh):
    parts = jax.sharding.Mesh(mesh.devices.reshape(4, 2, 2, 4, 2), ROW + COL)
    placed = (P(ROW, COL, None), P(ROW, COL), P(), P(), P(), P(), P(), P(), P(), P(), P())
    return jax.shard_map(
        body, mesh=parts, in_specs=placed, out_specs=P(ROW, COL, None), check_vma=False
    )
```
